32 devices in a mesh: row: 4 (over y, x), col: 8 (over z, core).
Axes of the slice: x: 2, y: 2, z: 4, core: 2. Of those that a mesh axis runs over, the one named last changes fastest.
Arguments:
- distances: float32 [1024, 1024], P('row', 'col'), may hold values from 0.5 to 8
- neighbor_ids: int32 [10, 1024], replicated, may hold values from 0 to 1023
- edge_lengths: float32 [10, 1024], P(None, ('row', 'col')), may hold values from 0.125 to 1
- pivots: int32 [2], replicated, may hold values from 0 to 31
Outputs:
- geodesic: float32 [1024, 1024], P('row', 'col')
The draws below stay inside these ranges and needn't reach their ends.
All inputs are finite; a program needn't handle non-finite values.
Results may differ from the reference program's by a relative error of at most 0.00002.
Values sent between devices are 32-bit elements; how exact they have to be, the bound alone decides.
A program may use at most 64 MiB of HBM per device.

```python
import jax
import jax.numpy as jnp
from jax import lax

NEIGHBORS = 10
PIVOT = 32
NV = 1024
BLOCKS = 32


def draw_distances(key, part):
    key = jax.random.fold_in(key, 11)
    unit = jax.random.uniform(key, (NV, NV), jnp.float32, 0.0, 1.0)
    return 0.5 + 7.5 * unit


def plant(values, own_key, least, largest):
    place = [jax.random.randint(jax.random.fold_in(own_key, axis), (), 0, length) for axis, length in enumerate(values.shape)]
    longest = values.shape.index(max(values.shape))
    beside = place[:longest] + [(place[longest] + 1) % values.shape[longest]] + place[longest + 1:]
    return values.at[tuple(place)].set(least).at[tuple(beside)].set(largest)


def block_levels(own_key, dims, shards, least, top_value):
    def one(position, blocks):
        steps = jax.random.uniform(jax.random.fold_in(jax.random.fold_in(own_key, 6), position), (blocks,), jnp.float32, least / len(shards), top_value / len(shards))
        return jnp.repeat(jnp.exp(steps), dims[position] // blocks).reshape((-1,) + (1,) * (len(dims) - position - 1))

    loudness = one(*shards[0])
    for cut in shards[1:]:
        loudness = loudness * one(*cut)
    return loudness


def setup_inputs(seed: int = 0) -> dict:
    seeds = jax.random.split(jax.random.key(seed), 5)
    distances = draw_distances(jax.random.fold_in(seeds[4], 71), 0)
    neighbor_ids = plant(jax.random.randint(seeds[1], (NEIGHBORS, NV), 0, NV), jax.random.fold_in(seeds[1], 1), 0, NV - 1).astype(jnp.int32)
    edge_lengths = jnp.clip(0.125 + 0.875 * jax.random.uniform(seeds[2], (NEIGHBORS, NV), jnp.float32) ** block_levels(seeds[2], (NEIGHBORS, NV), ((1, 32),), -0.2, 0.2), 0.125, 1.0)
    pivots = jax.random.randint(seeds[3], (2,), 0, BLOCKS).astype(jnp.int32)
    return {"distances": distances, "neighbor_ids": neighbor_ids, "edge_lengths": edge_lengths, "pivots": pivots}


def reference(distances, neighbor_ids, edge_lengths, pivots):
    vertex = jnp.arange(NV, dtype=jnp.int32)
    matrix = distances
    for k in range(NEIGHBORS):
        target = neighbor_ids[k].astype(jnp.int32)
        weight = edge_lengths[k]
        matrix = matrix.at[vertex, target].min(weight)
        matrix = matrix.at[target, vertex].min(weight)
    matrix = matrix.at[vertex, vertex].set(jnp.zeros((NV,), matrix.dtype))
    for q in range(2):
        base = (pivots[q] * PIVOT).astype(jnp.int32)

        def update(t, current):
            middle = (base + t).astype(jnp.int32)
            column = lax.dynamic_slice_in_dim(current, middle, 1, 1)
            row_line = lax.dynamic_slice_in_dim(current, middle, 1, 0)
            return jnp.minimum(current, column + row_line)

        matrix = lax.fori_loop(0, PIVOT, update, matrix)
    return matrix
```

```python
import functools

import jax
import jax.numpy as jnp
from jax import lax
from jax.experimental import pallas as pl
from jax.experimental.pallas import tpu as pltpu
from jax.sharding import PartitionSpec as P

NEIGHBORS = 10
PIVOT = 32
MESH = pl.DeviceIdType.MESH


def relax(block, row_ids, col_ids, ids_rows, len_rows, ids_cols, len_cols):
    for k in range(NEIGHBORS):
        forward = jnp.where(ids_rows[:, k : k + 1] == col_ids, len_rows[:, k : k + 1], jnp.inf)
        backward = jnp.where(row_ids == ids_cols[k : k + 1, :], len_cols[k : k + 1, :], jnp.inf)
        block = jnp.minimum(block, jnp.minimum(forward, backward))
    return jnp.where(row_ids == col_ids, jnp.float32(0.0), block)


def minplus(total, left, right):
    for k in range(left.shape[1]):
        term = left[:, k : k + 1] + right[k : k + 1, :]
        total = term if total is None else jnp.minimum(total, term)
    return total


def pick(items, index):
    chosen = items[0]
    index = jnp.full(chosen.shape, index, jnp.int32)
    for i in range(1, len(items)):
        chosen = jnp.where(index == i, items[i], chosen)
    return chosen


def kernel(nr, nc, pivots, dist, ids, lens, out,
           e_send, e_recv, e_all, e_t, c_send, c_recv, c_all, c_full,
           r_recv, k_recv, t_ref,
           es_sem, er_sem, rs_sem, rr_sem, cs_sem, cr_sem,
           ga_s, ga_r, ge_s, ge_r, ks_sem, kr_sem):
    rows_here, cols_here = dist.shape
    width = lens.shape[1]
    half = rows_here // 2
    piece = half // nc
    pair = 2 * PIVOT
    r, c = lax.axis_index("row"), lax.axis_index("col")
    row_peers = [lax.rem(r + i, nr) for i in range(1, nr)]
    col_peers = [lax.rem(c + i, nc) for i in range(1, nc)]

    barrier = pltpu.get_barrier_semaphore()
    for peer in row_peers:
        pl.semaphore_signal(barrier, inc=1, device_id=(peer, c), device_id_type=MESH)
    for peer in col_peers:
        pl.semaphore_signal(barrier, inc=1, device_id=(r, peer), device_id_type=MESH)

    p = [pivots[q] for q in range(2)]
    base = [p[q] * PIVOT for q in range(2)]
    row_root = [lax.div(base[q], rows_here) for q in range(2)]
    col_root = [lax.div(base[q], cols_here) for q in range(2)]
    row_slot = [lax.rem(p[q], rows_here // PIVOT) for q in range(2)]
    col_slot = [lax.rem(p[q], cols_here // PIVOT) for q in range(2)]
    row_cuts = [slice(i, i + PIVOT) for i in range(0, rows_here, PIVOT)]
    col_cuts = [slice(i, i + PIVOT) for i in range(0, cols_here, PIVOT)]

    own_len = lens[...]
    e_send[0:NEIGHBORS, :] = jnp.concatenate([own_len] * nr, axis=1)
    e_send[NEIGHBORS:16, :] = jnp.zeros((16 - NEIGHBORS, cols_here), jnp.float32)
    e_recv[r] = e_send[...]
    for q in range(2):
        r_recv[r, q * PIVOT : (q + 1) * PIVOT, :] = pick([dist[cut, :] for cut in row_cuts], row_slot[q])
    groups = cols_here // PIVOT
    lane = lax.broadcasted_iota(jnp.int32, (1, cols_here), 1)
    source = jnp.where(
        lane // PIVOT % 2 == 0, jnp.full_like(lane, col_slot[0]), jnp.full_like(lane, col_slot[1]))
    turn = (lane // PIVOT - source + groups) % groups
    packed = jnp.zeros((half, cols_here), jnp.float32)
    for h in range(2):
        part = dist[h * half : (h + 1) * half, :]
        for g in range(groups):
            turned = pltpu.roll(part, g * PIVOT, 1) if g else part
            packed = jnp.where((turn == g) & (lane // pair == h), turned, packed)
    for j in range(nc):
        c_send[j] = packed[j * piece : (j + 1) * piece, :]
    c_recv[c] = c_send[c]

    pl.semaphore_wait(barrier, nr + nc - 2)

    def send(src, dst, send_sem, recv_sem, peer):
        copy = pltpu.make_async_remote_copy(
            src_ref=src, dst_ref=dst, send_sem=send_sem, recv_sem=recv_sem,
            device_id=peer, device_id_type=MESH)
        copy.start()
        return copy

    def arrive(slot, sem, peer):
        pltpu.make_async_remote_copy(
            src_ref=slot, dst_ref=slot, send_sem=sem, recv_sem=sem,
            device_id=peer, device_id_type=MESH).wait_recv()

    sent = []
    for i, peer in enumerate(col_peers):
        sent.append(send(c_send.at[peer], c_recv.at[c], cs_sem.at[i], cr_sem.at[c], (r, peer)))
    for i, peer in enumerate(row_peers):
        sent.append(send(e_send, e_recv.at[r], es_sem.at[i], er_sem.at[r], (peer, c)))
    for i, peer in enumerate(row_peers):
        sent.append(send(r_recv.at[r], r_recv.at[r], rs_sem.at[i], rr_sem.at[r], (peer, c)))

    ids_rows = []
    for t in range(rows_here // cols_here):
        start = pl.multiple_of(r * rows_here + t * cols_here, cols_here)
        ids_rows.append(ids[:, pl.ds(start, cols_here)].T)
    ids_rows = jnp.concatenate(ids_rows, axis=0)
    ids_cols = ids[:, pl.ds(pl.multiple_of(c * cols_here, cols_here), cols_here)]
    ids_p = []
    id_tiles = [ids[:, j * cols_here : (j + 1) * cols_here] for j in range(nc)]
    for q in range(2):
        turned = pick(id_tiles, col_root[q]).T
        ids_p.append(pick([turned[cut, :] for cut in col_cuts], col_slot[q]))
    ids_p = jnp.concatenate(ids_p, axis=0)

    for peer in row_peers:
        arrive(e_recv.at[peer], er_sem.at[peer], (peer, c))
    lane_e = lax.broadcasted_iota(jnp.int32, (16, cols_here), 1)
    edges = e_recv[0]
    for i in range(1, nr):
        edges = jnp.where(lane_e // width == i, e_recv[i], edges)
    e_all[c] = edges
    for i, peer in enumerate(col_peers):
        sent.append(send(e_all.at[c], e_all.at[c], ge_s.at[i], ge_r.at[c], (r, peer)))
    for peer in col_peers:
        arrive(c_recv.at[peer], cr_sem.at[peer], (r, peer))
    lane_c = lax.broadcasted_iota(jnp.int32, (piece, cols_here), 1)
    c_all[c] = jnp.where(lane_c % pair < PIVOT,
                         pick([c_recv[j] for j in range(nc)], col_root[0]),
                         pick([c_recv[j] for j in range(nc)], col_root[1]))
    for i, peer in enumerate(col_peers):
        sent.append(send(c_all.at[c], c_all.at[c], ga_s.at[i], ga_r.at[c], (r, peer)))

    for peer in col_peers:
        arrive(c_all.at[peer], ga_r.at[peer], (r, peer))
    cols_packed = jnp.concatenate([c_all[j] for j in range(nc)], axis=0)
    c_full[0:half, :] = cols_packed
    c_full[half:rows_here, :] = pltpu.roll(cols_packed, pair, 1)
    cuts = [c_full[cut, :] for cut in row_cuts]
    first = pick(cuts, row_slot[0])
    second = pltpu.roll(pick(cuts, row_slot[1]), pair, 1)
    lane_k = lax.broadcasted_iota(jnp.int32, (PIVOT, cols_here), 1)
    k_recv[r] = jnp.where(lane_k < pair, first, second)
    for i, peer in enumerate(row_peers):
        sent.append(send(k_recv.at[r], k_recv.at[r], ks_sem.at[i], kr_sem.at[r], (peer, c)))

    for peer in col_peers:
        arrive(e_all.at[peer], ge_r.at[peer], (r, peer))
    for j in range(nc):
        e_t[j] = e_all[j].T

    def lengths_of(index):
        start = pl.multiple_of(index // nc * width, width)
        return e_t[index % nc, pl.ds(start, width), :]

    len_rows = jnp.concatenate([lengths_of(r * nc + j) for j in range(nc)], axis=0)
    len_cols = jnp.concatenate([lengths_of(c * nr + j) for j in range(nr)], axis=0).T
    steps = PIVOT // width
    len_p = []
    tiles = [e_all[j] for j in range(nc)]
    for index in [p[q] * steps + j for q in range(2) for j in range(steps)]:
        turned = pick(tiles, lax.rem(index, nc)).T
        len_p.append(pick([turned[i * width : (i + 1) * width, :] for i in range(nr)],
                          lax.div(index, nc)))
    len_p = jnp.concatenate(len_p, axis=0)
    ids_p_cols = ids_p.T
    len_p_cols = len_p.T

    row_ids = r * rows_here + lax.broadcasted_iota(jnp.int32, (rows_here, 1), 0)
    col_ids = c * cols_here + lax.broadcasted_iota(jnp.int32, (1, cols_here), 1)
    at_s = lax.broadcasted_iota(jnp.int32, (pair, 1), 0)
    p_rows = jnp.where(at_s < PIVOT, base[0] + at_s, base[1] + at_s - PIVOT)
    at_l = lax.broadcasted_iota(jnp.int32, (1, pair), 1)
    p_cols = jnp.where(at_l < PIVOT, base[0] + at_l, base[1] + at_l - PIVOT)

    for peer in row_peers:
        arrive(r_recv.at[peer], rr_sem.at[peer], (peer, c))
    rows_panel = jnp.concatenate(
        [pick([r_recv[i, q * PIVOT : (q + 1) * PIVOT, :] for i in range(nr)], row_root[q])
         for q in range(2)], axis=0)
    rows_panel = relax(rows_panel, p_rows, col_ids, ids_p, len_p, ids_cols, len_cols)
    out[...] = relax(dist[...], row_ids, col_ids, ids_rows, len_rows, ids_cols, len_cols)
    c_full[:, 0:pair] = relax(
        c_full[:, 0:pair], row_ids, p_cols, ids_rows, len_rows, ids_p_cols, len_p_cols)

    for peer in row_peers:
        arrive(k_recv.at[peer], kr_sem.at[peer], (peer, c))
    corner = jnp.concatenate(
        [pick([k_recv[i] for i in range(nr)], row_root[q])[:, q * pair : (q + 1) * pair]
         for q in range(2)], axis=0)
    corner = relax(corner, p_rows, p_cols, ids_p, len_p, ids_p_cols, len_p_cols)
    corner = lax.fori_loop(0, 6, lambda _, a: minplus(None, a, a), corner)
    t_ref[...] = minplus(None, corner, rows_panel)

    def finish(b, carry):
        at = pl.ds(pl.multiple_of(b * PIVOT, PIVOT), PIVOT)
        out[at, :] = minplus(out[at, :], c_full[at, 0:pair], t_ref[...])
        return carry

    lax.fori_loop(0, rows_here // PIVOT, finish, 0)
    for copy in sent:
        copy.wait_send()


def on_device(nr, nc, distances, neighbor_ids, edge_lengths, pivots):
    rows_here, cols_here = distances.shape
    half = rows_here // 2
    piece = half // nc
    vmem = pl.BlockSpec(memory_space=pltpu.VMEM)
    f32 = jnp.float32
    dma = pltpu.SemaphoreType.DMA
    return pl.pallas_call(
        functools.partial(kernel, nr, nc),
        out_shape=jax.ShapeDtypeStruct(distances.shape, f32),
        in_specs=[pl.BlockSpec(memory_space=pltpu.SMEM), vmem, vmem, vmem],
        out_specs=vmem,
        scratch_shapes=[
            pltpu.VMEM((16, cols_here), f32),
            pltpu.VMEM((nr, 16, cols_here), f32),
            pltpu.VMEM((nc, 16, cols_here), f32),
            pltpu.VMEM((nc, cols_here, 16), f32),
            pltpu.VMEM((nc, piece, cols_here), f32),
            pltpu.VMEM((nc, piece, cols_here), f32),
            pltpu.VMEM((nc, piece, cols_here), f32),
            pltpu.VMEM((rows_here, cols_here), f32),
            pltpu.VMEM((nr, 2 * PIVOT, cols_here), f32),
            pltpu.VMEM((nr, PIVOT, cols_here), f32),
            pltpu.VMEM((2 * PIVOT, cols_here), f32),
            dma((nr,)), dma((nr,)), dma((nr,)), dma((nr,)), dma((nc,)), dma((nc,)),
            dma((nc,)), dma((nc,)), dma((nc,)), dma((nc,)), dma((nr,)), dma((nr,)),
        ],
        compiler_params=pltpu.CompilerParams(
            collective_id=0, has_side_effects=True, vmem_limit_bytes=32 * 1024 * 1024),
    )(pivots, distances, neighbor_ids, edge_lengths)


def solution(mesh):
    placed = (P("row", "col"), P(), P(None, ("row", "col")), P())
    body = functools.partial(on_device, mesh.shape["row"], mesh.shape["col"])
    return jax.shard_map(
        body, mesh=mesh, in_specs=placed, out_specs=P("row", "col"), check_vma=False
    )
```

```python
import functools

import jax
import jax.numpy as jnp
from jax import lax
from jax.experimental import pallas as pl
from jax.experimental.pallas import tpu as pltpu
from jax.sharding import PartitionSpec as P

NEIGHBORS = 10
PIVOT = 32
MESH = pl.DeviceIdType.MESH


def relax(block, row_ids, col_ids, ids_rows, len_rows, ids_cols, len_cols):
    for k in range(NEIGHBORS):
        forward = jnp.where(ids_rows[:, k : k + 1] == col_ids, len_rows[:, k : k + 1], jnp.inf)
        backward = jnp.where(row_ids == ids_cols[k : k + 1, :], len_cols[k : k + 1, :], jnp.inf)
        block = jnp.minimum(block, jnp.minimum(forward, backward))
    return jnp.where(row_ids == col_ids, jnp.float32(0.0), block)


def minplus(total, left, right):
    for k in range(left.shape[1]):
        term = left[:, k : k + 1] + right[k : k + 1, :]
        total = term if total is None else jnp.minimum(total, term)
    return total


def pick(items, index):
    chosen = items[0]
    index = jnp.full(chosen.shape, index, jnp.int32)
    for i in range(1, len(items)):
        chosen = jnp.where(index == i, items[i], chosen)
    return chosen


def kernel(nr, nc, pivots_in, dist_in, ids_in, lens_in, out, pivots, dist, ids, lens, in_sem,
           e_send, e_recv, e_all, e_t, c_send, c_recv, c_all, c_full,
           r_recv, k_recv, t_ref,
           es_sem, er_sem, rs_sem, rr_sem, cs_sem, cr_sem,
           ga_s, ga_r, ge_s, ge_r, ks_sem, kr_sem):
    rows_here, cols_here = dist.shape
    width = lens.shape[1]
    half = rows_here // 2
    piece = half // nc
    pair = 2 * PIVOT
    r, c = lax.axis_index("row"), lax.axis_index("col")
    row_peers = [lax.rem(r + i, nr) for i in range(1, nr)]
    col_peers = [lax.rem(c + i, nc) for i in range(1, nc)]

    loads = [
        pltpu.make_async_copy(src, dst, in_sem.at[i])
        for i, (src, dst) in enumerate(
            [(pivots_in, pivots), (dist_in, dist), (lens_in, lens), (ids_in, ids)])
    ]
    for load in loads:
        load.start()

    barrier = pltpu.get_barrier_semaphore()
    for peer in row_peers:
        pl.semaphore_signal(barrier, inc=1, device_id=(peer, c), device_id_type=MESH)
    for peer in col_peers:
        pl.semaphore_signal(barrier, inc=1, device_id=(r, peer), device_id_type=MESH)

    for load in loads:
        load.wait()
    p = [pivots[q] for q in range(2)]
    base = [p[q] * PIVOT for q in range(2)]
    row_root = [lax.div(base[q], rows_here) for q in range(2)]
    col_root = [lax.div(base[q], cols_here) for q in range(2)]
    row_slot = [lax.rem(p[q], rows_here // PIVOT) for q in range(2)]
    col_slot = [lax.rem(p[q], cols_here // PIVOT) for q in range(2)]
    row_cuts = [slice(i, i + PIVOT) for i in range(0, rows_here, PIVOT)]
    col_cuts = [slice(i, i + PIVOT) for i in range(0, cols_here, PIVOT)]

    own_len = lens[...]
    e_send[0:NEIGHBORS, :] = jnp.concatenate([own_len] * nr, axis=1)
    e_send[NEIGHBORS:16, :] = jnp.zeros((16 - NEIGHBORS, cols_here), jnp.float32)
    e_recv[r] = e_send[...]
    for q in range(2):
        r_recv[r, q * PIVOT : (q + 1) * PIVOT, :] = pick([dist[cut, :] for cut in row_cuts], row_slot[q])
    groups = cols_here // PIVOT
    lane = lax.broadcasted_iota(jnp.int32, (1, cols_here), 1)
    source = jnp.where(
        lane // PIVOT % 2 == 0, jnp.full_like(lane, col_slot[0]), jnp.full_like(lane, col_slot[1]))
    turn = (lane // PIVOT - source + groups) % groups
    packed = jnp.zeros((half, cols_here), jnp.float32)
    for h in range(2):
        part = dist[h * half : (h + 1) * half, :]
        for g in range(groups):
            turned = pltpu.roll(part, g * PIVOT, 1) if g else part
            packed = jnp.where((turn == g) & (lane // pair == h), turned, packed)
    for j in range(nc):
        c_send[j] = packed[j * piece : (j + 1) * piece, :]
    c_recv[c] = c_send[c]

    pl.semaphore_wait(barrier, nr + nc - 2)

    def send(src, dst, send_sem, recv_sem, peer):
        copy = pltpu.make_async_remote_copy(
            src_ref=src, dst_ref=dst, send_sem=send_sem, recv_sem=recv_sem,
            device_id=peer, device_id_type=MESH)
        copy.start()
        return copy

    def arrive(slot, sem, peer):
        pltpu.make_async_remote_copy(
            src_ref=slot, dst_ref=slot, send_sem=sem, recv_sem=sem,
            device_id=peer, device_id_type=MESH).wait_recv()

    sent = []
    for i, peer in enumerate(col_peers):
        sent.append(send(c_send.at[peer], c_recv.at[c], cs_sem.at[i], cr_sem.at[c], (r, peer)))
    for i, peer in enumerate(row_peers):
        sent.append(send(e_send, e_recv.at[r], es_sem.at[i], er_sem.at[r], (peer, c)))
    for i, peer in enumerate(row_peers):
        sent.append(send(r_recv.at[r], r_recv.at[r], rs_sem.at[i], rr_sem.at[r], (peer, c)))

    ids_rows = []
    for t in range(rows_here // cols_here):
        start = pl.multiple_of(r * rows_here + t * cols_here, cols_here)
        ids_rows.append(ids[:, pl.ds(start, cols_here)].T)
    ids_rows = jnp.concatenate(ids_rows, axis=0)
    ids_cols = ids[:, pl.ds(pl.multiple_of(c * cols_here, cols_here), cols_here)]
    ids_p = []
    id_tiles = [ids[:, j * cols_here : (j + 1) * cols_here] for j in range(nc)]
    for q in range(2):
        turned = pick(id_tiles, col_root[q]).T
        ids_p.append(pick([turned[cut, :] for cut in col_cuts], col_slot[q]))
    ids_p = jnp.concatenate(ids_p, axis=0)

    for peer in row_peers:
        arrive(e_recv.at[peer], er_sem.at[peer], (peer, c))
    lane_e = lax.broadcasted_iota(jnp.int32, (16, cols_here), 1)
    edges = e_recv[0]
    for i in range(1, nr):
        edges = jnp.where(lane_e // width == i, e_recv[i], edges)
    e_all[c] = edges
    for i, peer in enumerate(col_peers):
        sent.append(send(e_all.at[c], e_all.at[c], ge_s.at[i], ge_r.at[c], (r, peer)))
    for peer in col_peers:
        arrive(c_recv.at[peer], cr_sem.at[peer], (r, peer))
    lane_c = lax.broadcasted_iota(jnp.int32, (piece, cols_here), 1)
    c_all[c] = jnp.where(lane_c % pair < PIVOT,
                         pick([c_recv[j] for j in range(nc)], col_root[0]),
                         pick([c_recv[j] for j in range(nc)], col_root[1]))
    for i, peer in enumerate(col_peers):
        sent.append(send(c_all.at[c], c_all.at[c], ga_s.at[i], ga_r.at[c], (r, peer)))

    for peer in col_peers:
        arrive(c_all.at[peer], ga_r.at[peer], (r, peer))
    cols_packed = jnp.concatenate([c_all[j] for j in range(nc)], axis=0)
    c_full[0:half, :] = cols_packed
    c_full[half:rows_here, :] = pltpu.roll(cols_packed, pair, 1)
    cuts = [c_full[cut, :] for cut in row_cuts]
    first = pick(cuts, row_slot[0])
    second = pltpu.roll(pick(cuts, row_slot[1]), pair, 1)
    lane_k = lax.broadcasted_iota(jnp.int32, (PIVOT, cols_here), 1)
    k_recv[r] = jnp.where(lane_k < pair, first, second)
    for i, peer in enumerate(row_peers):
        sent.append(send(k_recv.at[r], k_recv.at[r], ks_sem.at[i], kr_sem.at[r], (peer, c)))

    for peer in col_peers:
        arrive(e_all.at[peer], ge_r.at[peer], (r, peer))
    for j in range(nc):
        e_t[j] = e_all[j].T

    def lengths_of(index):
        start = pl.multiple_of(index // nc * width, width)
        return e_t[index % nc, pl.ds(start, width), :]

    len_rows = jnp.concatenate([lengths_of(r * nc + j) for j in range(nc)], axis=0)
    len_cols = jnp.concatenate([lengths_of(c * nr + j) for j in range(nr)], axis=0).T
    steps = PIVOT // width
    len_p = []
    tiles = [e_all[j] for j in range(nc)]
    for index in [p[q] * steps + j for q in range(2) for j in range(steps)]:
        turned = pick(tiles, lax.rem(index, nc)).T
        len_p.append(pick([turned[i * width : (i + 1) * width, :] for i in range(nr)],
                          lax.div(index, nc)))
    len_p = jnp.concatenate(len_p, axis=0)
    ids_p_cols = ids_p.T
    len_p_cols = len_p.T

    row_ids = r * rows_here + lax.broadcasted_iota(jnp.int32, (rows_here, 1), 0)
    col_ids = c * cols_here + lax.broadcasted_iota(jnp.int32, (1, cols_here), 1)
    at_s = lax.broadcasted_iota(jnp.int32, (pair, 1), 0)
    p_rows = jnp.where(at_s < PIVOT, base[0] + at_s, base[1] + at_s - PIVOT)
    at_l = lax.broadcasted_iota(jnp.int32, (1, pair), 1)
    p_cols = jnp.where(at_l < PIVOT, base[0] + at_l, base[1] + at_l - PIVOT)

    for peer in row_peers:
        arrive(r_recv.at[peer], rr_sem.at[peer], (peer, c))
    rows_panel = jnp.concatenate(
        [pick([r_recv[i, q * PIVOT : (q + 1) * PIVOT, :] for i in range(nr)], row_root[q])
         for q in range(2)], axis=0)
    rows_panel = relax(rows_panel, p_rows, col_ids, ids_p, len_p, ids_cols, len_cols)
    out[...] = relax(dist[...], row_ids, col_ids, ids_rows, len_rows, ids_cols, len_cols)
    c_full[:, 0:pair] = relax(
        c_full[:, 0:pair], row_ids, p_cols, ids_rows, len_rows, ids_p_cols, len_p_cols)

    for peer in row_peers:
        arrive(k_recv.at[peer], kr_sem.at[peer], (peer, c))
    corner = jnp.concatenate(
        [pick([k_recv[i] for i in range(nr)], row_root[q])[:, q * pair : (q + 1) * pair]
         for q in range(2)], axis=0)
    corner = relax(corner, p_rows, p_cols, ids_p, len_p, ids_p_cols, len_p_cols)
    corner = lax.fori_loop(0, 6, lambda _, a: minplus(None, a, a), corner)
    t_ref[...] = minplus(None, corner, rows_panel)

    def finish(b, carry):
        at = pl.ds(pl.multiple_of(b * PIVOT, PIVOT), PIVOT)
        out[at, :] = minplus(out[at, :], c_full[at, 0:pair], t_ref[...])
        return carry

    lax.fori_loop(0, rows_here // PIVOT, finish, 0)
    for copy in sent:
        copy.wait_send()


def on_device(nr, nc, distances, neighbor_ids, edge_lengths, pivots):
    rows_here, cols_here = distances.shape
    half = rows_here // 2
    piece = half // nc
    vmem = pl.BlockSpec(memory_space=pltpu.VMEM)
    f32 = jnp.float32
    dma = pltpu.SemaphoreType.DMA
    return pl.pallas_call(
        functools.partial(kernel, nr, nc),
        out_shape=jax.ShapeDtypeStruct(distances.shape, f32),
        in_specs=[pl.BlockSpec(memory_space=pltpu.HBM)] * 4,
        out_specs=vmem,
        scratch_shapes=[
            pltpu.SMEM(pivots.shape, jnp.int32),
            pltpu.VMEM(distances.shape, f32),
            pltpu.VMEM(neighbor_ids.shape, jnp.int32),
            pltpu.VMEM(edge_lengths.shape, f32),
            dma((4,)),
            pltpu.VMEM((16, cols_here), f32),
            pltpu.VMEM((nr, 16, cols_here), f32),
            pltpu.VMEM((nc, 16, cols_here), f32),
            pltpu.VMEM((nc, cols_here, 16), f32),
            pltpu.VMEM((nc, piece, cols_here), f32),
            pltpu.VMEM((nc, piece, cols_here), f32),
            pltpu.VMEM((nc, piece, cols_here), f32),
            pltpu.VMEM((rows_here, cols_here), f32),
            pltpu.VMEM((nr, 2 * PIVOT, cols_here), f32),
            pltpu.VMEM((nr, PIVOT, cols_here), f32),
            pltpu.VMEM((2 * PIVOT, cols_here), f32),
            dma((nr,)), dma((nr,)), dma((nr,)), dma((nr,)), dma((nc,)), dma((nc,)),
            dma((nc,)), dma((nc,)), dma((nc,)), dma((nc,)), dma((nr,)), dma((nr,)),
        ],
        compiler_params=pltpu.CompilerParams(
            collective_id=0, has_side_effects=True, vmem_limit_bytes=32 * 1024 * 1024),
    )(pivots, distances, neighbor_ids, edge_lengths)


def solution(mesh):
    placed = (P("row", "col"), P(), P(None, ("row", "col")), P())
    body = functools.partial(on_device, mesh.shape["row"], mesh.shape["col"])
    return jax.shard_map(
        body, mesh=mesh, in_specs=placed, out_specs=P("row", "col"), check_vma=False
    )
```

```python
import functools

import jax
import jax.numpy as jnp
from jax import lax
from jax.experimental import pallas as pl
from jax.experimental.pallas import tpu as pltpu
from jax.sharding import PartitionSpec as P

NEIGHBORS = 10
PIVOT = 32
MESH = pl.DeviceIdType.MESH


def relax(block, row_ids, col_ids, ids_rows, len_rows, ids_cols, len_cols):
    for k in range(NEIGHBORS):
        forward = jnp.where(ids_rows[:, k : k + 1] == col_ids, len_rows[:, k : k + 1], jnp.inf)
        backward = jnp.where(row_ids == ids_cols[k : k + 1, :], len_cols[k : k + 1, :], jnp.inf)
        block = jnp.minimum(block, jnp.minimum(forward, backward))
    return jnp.where(row_ids == col_ids, jnp.float32(0.0), block)


def minplus(total, left, right):
    for k in range(left.shape[1]):
        term = left[:, k : k + 1] + right[k : k + 1, :]
        total = term if total is None else jnp.minimum(total, term)
    return total


def pick(items, index):
    chosen = items[0]
    index = jnp.full(chosen.shape, index, jnp.int32)
    for i in range(1, len(items)):
        chosen = jnp.where(index == i, items[i], chosen)
    return chosen


def kernel(nr, nc, pivots_in, dist_in, ids_in, lens_in, out, pivots, dist, ids, lens, in_sem,
           e_send, e_recv, e_all, e_t, c_send, c_recv, c_all, c_full,
           r_recv, k_recv, t_ref,
           es_sem, er_sem, rs_sem, rr_sem, cs_sem, cr_sem,
           ga_s, ga_r, ge_s, ge_r, ks_sem, kr_sem):
    rows_here, cols_here = dist.shape
    width = lens.shape[1]
    half = rows_here // 2
    piece = half // nc
    pair = 2 * PIVOT
    r, c = lax.axis_index("row"), lax.axis_index("col")
    row_peers = [lax.rem(r + i, nr) for i in range(1, nr)]
    col_peers = [lax.rem(c + i, nc) for i in range(1, nc)]

    loads = [
        pltpu.make_async_copy(src, dst, in_sem.at[i])
        for i, (src, dst) in enumerate(
            [(pivots_in, pivots), (dist_in, dist), (lens_in, lens), (ids_in, ids)])
    ]
    for load in loads:
        load.start()

    barrier = pltpu.get_barrier_semaphore()
    for peer in row_peers:
        pl.semaphore_signal(barrier, inc=1, device_id=(peer, c), device_id_type=MESH)
    for peer in col_peers:
        pl.semaphore_signal(barrier, inc=1, device_id=(r, peer), device_id_type=MESH)

    for load in loads:
        load.wait()
    p = [pivots[q] for q in range(2)]
    base = [p[q] * PIVOT for q in range(2)]
    row_root = [lax.div(base[q], rows_here) for q in range(2)]
    col_root = [lax.div(base[q], cols_here) for q in range(2)]
    row_slot = [lax.rem(p[q], rows_here // PIVOT) for q in range(2)]
    col_slot = [lax.rem(p[q], cols_here // PIVOT) for q in range(2)]
    row_cuts = [slice(i, i + PIVOT) for i in range(0, rows_here, PIVOT)]
    col_cuts = [slice(i, i + PIVOT) for i in range(0, cols_here, PIVOT)]

    own_len = lens[...]
    e_send[0:NEIGHBORS, :] = jnp.concatenate([own_len] * nr, axis=1)
    e_send[NEIGHBORS:16, :] = jnp.zeros((16 - NEIGHBORS, cols_here), jnp.float32)
    e_recv[r] = e_send[...]
    for q in range(2):
        r_recv[r, q * PIVOT : (q + 1) * PIVOT, :] = pick([dist[cut, :] for cut in row_cuts], row_slot[q])
    groups = cols_here // PIVOT
    lane = lax.broadcasted_iota(jnp.int32, (1, cols_here), 1)
    source = jnp.where(
        lane // PIVOT % 2 == 0, jnp.full_like(lane, col_slot[0]), jnp.full_like(lane, col_slot[1]))
    turn = (lane // PIVOT - source + groups) % groups
    packed = jnp.zeros((half, cols_here), jnp.float32)
    for h in range(2):
        part = dist[h * half : (h + 1) * half, :]
        for g in range(groups):
            turned = pltpu.roll(part, g * PIVOT, 1) if g else part
            packed = jnp.where((turn == g) & (lane // pair == h), turned, packed)
    for j in range(nc):
        c_send[j] = packed[j * piece : (j + 1) * piece, :]
    c_recv[c] = c_send[c]

    pl.semaphore_wait(barrier, nr + nc - 2)

    def send(src, dst, send_sem, recv_sem, peer):
        copy = pltpu.make_async_remote_copy(
            src_ref=src, dst_ref=dst, send_sem=send_sem, recv_sem=recv_sem,
            device_id=peer, device_id_type=MESH)
        copy.start()
        return copy

    def arrive(slot, sem, peer):
        pltpu.make_async_remote_copy(
            src_ref=slot, dst_ref=slot, send_sem=sem, recv_sem=sem,
            device_id=peer, device_id_type=MESH).wait_recv()

    sent = []
    for i, peer in enumerate(col_peers):
        sent.append(send(c_send.at[peer], c_recv.at[c], cs_sem.at[i], cr_sem.at[c], (r, peer)))
    for i, peer in enumerate(row_peers):
        sent.append(send(e_send, e_recv.at[r], es_sem.at[i], er_sem.at[r], (peer, c)))
    for i, peer in enumerate(row_peers):
        sent.append(send(r_recv.at[r], r_recv.at[r], rs_sem.at[i], rr_sem.at[r], (peer, c)))

    ids_rows = []
    for t in range(rows_here // cols_here):
        start = pl.multiple_of(r * rows_here + t * cols_here, cols_here)
        ids_rows.append(ids[:, pl.ds(start, cols_here)].T)
    ids_rows = jnp.concatenate(ids_rows, axis=0)
    ids_cols = ids[:, pl.ds(pl.multiple_of(c * cols_here, cols_here), cols_here)]
    ids_p = []
    id_tiles = [ids[:, j * cols_here : (j + 1) * cols_here] for j in range(nc)]
    for q in range(2):
        turned = pick(id_tiles, col_root[q]).T
        ids_p.append(pick([turned[cut, :] for cut in col_cuts], col_slot[q]))
    ids_p = jnp.concatenate(ids_p, axis=0)

    for peer in row_peers:
        arrive(e_recv.at[peer], er_sem.at[peer], (peer, c))
    lane_e = lax.broadcasted_iota(jnp.int32, (16, cols_here), 1)
    edges = e_recv[0]
    for i in range(1, nr):
        edges = jnp.where(lane_e // width == i, e_recv[i], edges)
    e_all[c] = edges
    for i, peer in enumerate(col_peers):
        sent.append(send(e_all.at[c], e_all.at[c], ge_s.at[i], ge_r.at[c], (r, peer)))
    for peer in col_peers:
        arrive(c_recv.at[peer], cr_sem.at[peer], (r, peer))
    lane_c = lax.broadcasted_iota(jnp.int32, (piece, cols_here), 1)
    c_all[c] = jnp.where(lane_c % pair < PIVOT,
                         pick([c_recv[j] for j in range(nc)], col_root[0]),
                         pick([c_recv[j] for j in range(nc)], col_root[1]))
    for i, peer in enumerate(col_peers):
        sent.append(send(c_all.at[c], c_all.at[c], ga_s.at[i], ga_r.at[c], (r, peer)))

    for peer in col_peers:
        arrive(c_all.at[peer], ga_r.at[peer], (r, peer))
    cols_packed = jnp.concatenate([c_all[j] for j in range(nc)], axis=0)
    c_full[0:half, :] = cols_packed
    c_full[half:rows_here, :] = pltpu.roll(cols_packed, pair, 1)
    cuts = [c_full[cut, :] for cut in row_cuts]
    first = pick(cuts, row_slot[0])
    second = pltpu.roll(pick(cuts, row_slot[1]), pair, 1)
    lane_k = lax.broadcasted_iota(jnp.int32, (PIVOT, cols_here), 1)
    k_recv[r] = jnp.where(lane_k < pair, first, second)
    for i, peer in enumerate(row_peers):
        sent.append(send(k_recv.at[r], k_recv.at[r], ks_sem.at[i], kr_sem.at[r], (peer, c)))

    for peer in col_peers:
        arrive(e_all.at[peer], ge_r.at[peer], (r, peer))
    for j in range(nc):
        e_t[j] = e_all[j].T

    def lengths_of(index):
        start = pl.multiple_of(index // nc * width, width)
        return e_t[index % nc, pl.ds(start, width), :]

    len_rows = jnp.concatenate([lengths_of(r * nc + j) for j in range(nc)], axis=0)
    len_cols = jnp.concatenate([lengths_of(c * nr + j) for j in range(nr)], axis=0).T
    steps = PIVOT // width
    len_p = []
    tiles = [e_all[j] for j in range(nc)]
    for index in [p[q] * steps + j for q in range(2) for j in range(steps)]:
        turned = pick(tiles, lax.rem(index, nc)).T
        len_p.append(pick([turned[i * width : (i + 1) * width, :] for i in range(nr)],
                          lax.div(index, nc)))
    len_p = jnp.concatenate(len_p, axis=0)
    ids_p_cols = ids_p.T
    len_p_cols = len_p.T

    row_ids = r * rows_here + lax.broadcasted_iota(jnp.int32, (rows_here, 1), 0)
    col_ids = c * cols_here + lax.broadcasted_iota(jnp.int32, (1, cols_here), 1)
    at_s = lax.broadcasted_iota(jnp.int32, (pair, 1), 0)
    p_rows = jnp.where(at_s < PIVOT, base[0] + at_s, base[1] + at_s - PIVOT)
    at_l = lax.broadcasted_iota(jnp.int32, (1, pair), 1)
    p_cols = jnp.where(at_l < PIVOT, base[0] + at_l, base[1] + at_l - PIVOT)

    for peer in row_peers:
        arrive(r_recv.at[peer], rr_sem.at[peer], (peer, c))
    rows_panel = jnp.concatenate(
        [pick([r_recv[i, q * PIVOT : (q + 1) * PIVOT, :] for i in range(nr)], row_root[q])
         for q in range(2)], axis=0)
    rows_panel = relax(rows_panel, p_rows, col_ids, ids_p, len_p, ids_cols, len_cols)
    out[...] = relax(dist[...], row_ids, col_ids, ids_rows, len_rows, ids_cols, len_cols)
    c_full[:, 0:pair] = relax(
        c_full[:, 0:pair], row_ids, p_cols, ids_rows, len_rows, ids_p_cols, len_p_cols)

    for peer in row_peers:
        arrive(k_recv.at[peer], kr_sem.at[peer], (peer, c))
    corner = jnp.concatenate(
        [pick([k_recv[i] for i in range(nr)], row_root[q])[:, q * pair : (q + 1) * pair]
         for q in range(2)], axis=0)
    corner = relax(corner, p_rows, p_cols, ids_p, len_p, ids_p_cols, len_p_cols)
    corner = lax.fori_loop(0, 6, lambda _, a: minplus(None, a, a), corner)
    t_ref[...] = minplus(None, corner, rows_panel)

    def finish(b, carry):
        at = pl.ds(pl.multiple_of(b * PIVOT, PIVOT), PIVOT)
        out[at, :] = minplus(out[at, :], c_full[at, 0:pair], t_ref[...])
        return carry

    lax.fori_loop(0, rows_here // PIVOT, finish, 0)
    for copy in sent:
        copy.wait_send()


def on_device(nr, nc, distances, neighbor_ids, edge_lengths, pivots):
    rows_here, cols_here = distances.shape
    half = rows_here // 2
    piece = half // nc
    vmem = pl.BlockSpec(memory_space=pltpu.VMEM)
    f32 = jnp.float32
    dma = pltpu.SemaphoreType.DMA
    return pl.pallas_call(
        functools.partial(kernel, nr, nc),
        out_shape=jax.ShapeDtypeStruct(distances.shape, f32),
        in_specs=[pl.BlockSpec(memory_space=pltpu.HBM)] * 4,
        out_specs=vmem,
        scratch_shapes=[
            pltpu.SMEM(pivots.shape, jnp.int32),
            pltpu.VMEM(distances.shape, f32),
            pltpu.VMEM(neighbor_ids.shape, jnp.int32),
            pltpu.VMEM(edge_lengths.shape, f32),
            dma((4,)),
            pltpu.VMEM((16, cols_here), f32),
            pltpu.VMEM((nr, 16, cols_here), f32),
            pltpu.VMEM((nc, 16, cols_here), f32),
            pltpu.VMEM((nc, cols_here, 16), f32),
            pltpu.VMEM((nc, piece, cols_here), f32),
            pltpu.VMEM((nc, piece, cols_here), f32),
            pltpu.VMEM((nc, piece, cols_here), f32),
            pltpu.VMEM((rows_here, cols_here), f32),
            pltpu.VMEM((nr, 2 * PIVOT, cols_here), f32),
            pltpu.VMEM((nr, PIVOT, cols_here), f32),
            pltpu.VMEM((2 * PIVOT, cols_here), f32),
            dma((nr,)), dma((nr,)), dma((nr,)), dma((nr,)), dma((nc,)), dma((nc,)),
            dma((nc,)), dma((nc,)), dma((nc,)), dma((nc,)), dma((nr,)), dma((nr,)),
        ],
        compiler_params=pltpu.CompilerParams(
            collective_id=0, has_side_effects=True, vmem_limit_bytes=60 * 1024 * 1024),
    )(pivots, distances, neighbor_ids, edge_lengths)


def solution(mesh):
    placed = (P("row", "col"), P(), P(None, ("row", "col")), P())
    body = functools.partial(on_device, mesh.shape["row"], mesh.shape["col"])
    return jax.shard_map(
        body, mesh=mesh, in_specs=placed, out_specs=P("row", "col"), check_vma=False
    )
```

```python
import functools

import jax
import jax.numpy as jnp
from jax import lax
from jax.experimental import pallas as pl
from jax.experimental.pallas import tpu as pltpu
from jax.sharding import PartitionSpec as P

NEIGHBORS = 10
PIVOT = 32
MESH = pl.DeviceIdType.MESH


def edge_bound(row_ids, col_ids, ids_rows, len_rows, ids_cols, len_cols):
    bound = jnp.where(row_ids == col_ids, jnp.float32(0.0), jnp.inf)
    for k in range(NEIGHBORS):
        forward = jnp.where(ids_rows[:, k : k + 1] == col_ids, len_rows[:, k : k + 1], jnp.inf)
        backward = jnp.where(row_ids == ids_cols[k : k + 1, :], len_cols[k : k + 1, :], jnp.inf)
        bound = jnp.minimum(bound, jnp.minimum(forward, backward))
    return bound


def minplus(total, left, right):
    for k in range(left.shape[1]):
        term = left[:, k : k + 1] + right[k : k + 1, :]
        total = term if total is None else jnp.minimum(total, term)
    return total


def pick(items, index):
    chosen = items[0]
    index = jnp.full(chosen.shape, index, jnp.int32)
    for i in range(1, len(items)):
        chosen = jnp.where(index == i, items[i], chosen)
    return chosen


def kernel(nr, nc, pivots_in, dist_in, ids_in, lens_in, out, pivots, dist, ids, lens, in_sem,
           e_all, ids_r, len_r, c_send, c_recv, c_all, c_full, r_recv, k_recv, t_ref, sems):
    rows_here, cols_here = dist.shape
    width = lens.shape[1]
    depth = e_all.shape[1]
    groups = cols_here // width
    half = rows_here // 2
    piece = half // nc
    pair = 2 * PIVOT
    devices = nr * nc
    r, c = lax.axis_index("row"), lax.axis_index("col")
    me = r * nc + c
    row_peers = [lax.rem(r + i, nr) for i in range(1, nr)]
    col_peers = [lax.rem(c + i, nc) for i in range(1, nc)]

    loads = [
        pltpu.make_async_copy(src, dst, in_sem.at[i])
        for i, (src, dst) in enumerate(
            [(pivots_in, pivots), (dist_in, dist), (lens_in, lens), (ids_in, ids)])
    ]
    for load in loads:
        load.start()

    barrier = pltpu.get_barrier_semaphore()

    def greet(i, carry):
        other = lax.rem(me + i, devices)
        pl.semaphore_signal(barrier, inc=1, device_id=(lax.div(other, nc), lax.rem(other, nc)),
                            device_id_type=MESH)
        return carry

    lax.fori_loop(1, devices, greet, 0)

    for load in loads:
        load.wait()
    p = [pivots[q] for q in range(2)]
    base = [p[q] * PIVOT for q in range(2)]
    row_root = [lax.div(base[q], rows_here) for q in range(2)]
    col_root = [lax.div(base[q], cols_here) for q in range(2)]
    row_slot = [lax.rem(p[q], rows_here // PIVOT) for q in range(2)]
    col_slot = [lax.rem(p[q], cols_here // PIVOT) for q in range(2)]
    row_cuts = [slice(i, i + PIVOT) for i in range(0, rows_here, PIVOT)]

    blocks = cols_here // PIVOT
    lane = lax.broadcasted_iota(jnp.int32, (1, cols_here), 1)
    source = jnp.where(
        lane // PIVOT % 2 == 0, jnp.full_like(lane, col_slot[0]), jnp.full_like(lane, col_slot[1]))
    turn = (lane // PIVOT - source + blocks) % blocks
    packed = jnp.zeros((half, cols_here), jnp.float32)
    for h in range(2):
        part = dist[h * half : (h + 1) * half, :]
        for g in range(blocks):
            turned = pltpu.roll(part, g * PIVOT, 1) if g else part
            packed = jnp.where((turn == g) & (lane // pair == h), turned, packed)
    for j in range(nc):
        c_send[j] = packed[j * piece : (j + 1) * piece, :]
    c_recv[c] = c_send[c]
    own_len = jnp.concatenate(
        [lens[...], jnp.zeros((groups * depth - NEIGHBORS, width), jnp.float32)], axis=0)
    e_all[me] = jnp.concatenate(
        [own_len[g * depth : (g + 1) * depth, :] for g in range(groups)], axis=1)
    for q in range(2):
        r_recv[r, q * PIVOT : (q + 1) * PIVOT, :] = pick([dist[cut, :] for cut in row_cuts], row_slot[q])

    pl.semaphore_wait(barrier, devices - 1)

    def send(src, dst, kind, peer):
        pltpu.make_async_remote_copy(
            src_ref=src, dst_ref=dst, send_sem=sems.at[kind, 0], recv_sem=sems.at[kind, 1],
            device_id=peer, device_id_type=MESH).start()

    def all_of(buffer, kind):
        count = buffer.shape[0] - 1
        every = buffer.at[pl.ds(0, count)]
        return pltpu.make_async_remote_copy(
            src_ref=every, dst_ref=every, send_sem=sems.at[kind, 0], recv_sem=sems.at[kind, 1],
            device_id=(lax.rem(r + 1, nr), c), device_id_type=MESH)

    for peer in col_peers:
        send(c_send.at[peer], c_recv.at[c], 0, (r, peer))

    def send_edges(i, carry):
        other = lax.rem(me + i, devices)
        send(e_all.at[me], e_all.at[me], 1, (lax.div(other, nc), lax.rem(other, nc)))
        return carry

    lax.fori_loop(1, devices, send_edges, 0)
    for peer in row_peers:
        send(r_recv.at[r], r_recv.at[r], 2, (peer, c))

    for t in range(0, rows_here, cols_here):
        start = pl.multiple_of(r * rows_here + t, cols_here)
        ids_r[t : t + cols_here, :] = ids[:, pl.ds(start, cols_here)].T
    ids_own = ids[:, pl.ds(pl.multiple_of(c * cols_here, cols_here), cols_here)]
    id_tiles = [ids[:, j * cols_here : (j + 1) * cols_here] for j in range(nc)]
    mixed = jnp.zeros_like(ids_own)
    for q in range(2):
        tile = pick(id_tiles, col_root[q])
        for g in range(blocks):
            turned = pltpu.roll(tile, g * PIVOT, 1) if g else tile
            mixed = jnp.where((turn == g) & (lane // PIVOT == q), turned, mixed)
    ids_p = mixed.T[0:pair, :]
    ids_cols = jnp.concatenate([ids_own, mixed], axis=1)
    at_s = lax.broadcasted_iota(jnp.int32, (pair, 1), 0)
    p_rows = jnp.where(at_s < PIVOT, base[0] + at_s, base[1] + at_s - PIVOT)
    p_cols = jnp.where(lane < PIVOT, base[0] + lane, base[1] + lane - PIVOT)
    col_ids = jnp.concatenate([c * cols_here + lane, p_cols], axis=1)

    all_of(c_recv, 0).wait_recv()
    arrived = [c_recv[j] for j in range(nc)]
    c_all[c] = jnp.where(lane % pair < PIVOT, pick(arrived, col_root[0]), pick(arrived, col_root[1]))
    for peer in col_peers:
        send(c_all.at[c], c_all.at[c], 3, (r, peer))

    all_of(e_all, 1).wait_recv()

    def spread(tiles):
        parts = []
        for g in range(-(-NEIGHBORS // depth)):
            part = jnp.zeros((depth, cols_here), jnp.float32)
            for i, tile in enumerate(tiles):
                turned = pltpu.roll(tile, (i - g) * width % cols_here, 1) if i != g else tile
                part = jnp.where(lane // width == i, turned, part)
            parts.append(part)
        return jnp.concatenate(parts, axis=0)

    for t in range(0, rows_here, cols_here):
        len_r[t : t + cols_here, :] = spread(
            [e_all[r * nc + t // width + i] for i in range(groups)])[0:NEIGHBORS].T
    len_own = spread([e_all[c * nr + i] for i in range(nr)])
    steps = PIVOT // width
    everyone = [e_all[i] for i in range(devices)]
    len_mixed = spread([pick(everyone, p[q] * steps + j) for q in range(2) for j in range(steps)])
    len_p = len_mixed[0:NEIGHBORS].T[0:pair, :]
    len_cols = jnp.concatenate([len_own, len_mixed], axis=1)

    p_bound = edge_bound(p_rows, col_ids, ids_p, len_p, ids_cols, len_cols)
    all_of(r_recv, 2).wait_recv()
    rows_panel = jnp.concatenate(
        [pick([r_recv[i, q * PIVOT : (q + 1) * PIVOT, :] for i in range(nr)], row_root[q])
         for q in range(2)], axis=0)
    rows_panel = jnp.minimum(rows_panel, p_bound[:, 0:cols_here])

    all_of(c_all, 3).wait_recv()
    cols_packed = jnp.concatenate([c_all[j] for j in range(nc)], axis=0)
    c_full[0:half, :] = cols_packed
    c_full[half:rows_here, :] = pltpu.roll(cols_packed, pair, 1)
    cuts = [c_full[cut, :] for cut in row_cuts]
    second = pltpu.roll(pick(cuts, row_slot[1]), pair, 1)
    k_recv[r] = jnp.where(lane < pair, pick(cuts, row_slot[0]), second)
    for peer in row_peers:
        send(k_recv.at[r], k_recv.at[r], 4, (peer, c))

    def start_rows(b, carry):
        at = pl.ds(pl.multiple_of(b * PIVOT, PIVOT), PIVOT)
        row_ids = r * rows_here + b * PIVOT + lax.broadcasted_iota(jnp.int32, (PIVOT, 1), 0)
        bound = edge_bound(row_ids, col_ids, ids_r[at, :], len_r[at, :], ids_cols, len_cols)
        out[at, :] = jnp.minimum(dist[at, :], bound[:, 0:cols_here])
        c_full[at, :] = jnp.minimum(c_full[at, :], bound[:, cols_here:])
        return carry

    lax.fori_loop(0, rows_here // PIVOT, start_rows, 0)

    all_of(k_recv, 4).wait_recv()
    corner = jnp.concatenate(
        [pick([k_recv[i] for i in range(nr)], row_root[q])[:, q * pair : (q + 1) * pair]
         for q in range(2)], axis=0)
    corner = jnp.minimum(corner, p_bound[:, cols_here : cols_here + pair])
    corner = lax.fori_loop(0, 6, lambda _, a: minplus(None, a, a), corner)
    t_ref[...] = minplus(None, corner, rows_panel)

    def finish(b, carry):
        at = pl.ds(pl.multiple_of(b * PIVOT, PIVOT), PIVOT)
        out[at, :] = minplus(out[at, :], c_full[at, 0:pair], t_ref[...])
        return carry

    lax.fori_loop(0, rows_here // PIVOT, finish, 0)
    for kind, buffer in enumerate([c_recv, e_all, r_recv, c_all, k_recv]):
        all_of(buffer, kind).wait_send()


def on_device(nr, nc, distances, neighbor_ids, edge_lengths, pivots):
    rows_here, cols_here = distances.shape
    half = rows_here // 2
    piece = half // nc
    depth = pl.next_power_of_2(pl.cdiv(NEIGHBORS, cols_here // edge_lengths.shape[1]))
    vmem = pl.BlockSpec(memory_space=pltpu.VMEM)
    f32 = jnp.float32
    dma = pltpu.SemaphoreType.DMA
    return pl.pallas_call(
        functools.partial(kernel, nr, nc),
        out_shape=jax.ShapeDtypeStruct(distances.shape, f32),
        in_specs=[pl.BlockSpec(memory_space=pltpu.HBM)] * 4,
        out_specs=vmem,
        scratch_shapes=[
            pltpu.SMEM(pivots.shape, jnp.int32),
            pltpu.VMEM(distances.shape, f32),
            pltpu.VMEM(neighbor_ids.shape, jnp.int32),
            pltpu.VMEM(edge_lengths.shape, f32),
            dma((4,)),
            pltpu.VMEM((nr * nc, depth, cols_here), f32),
            pltpu.VMEM((rows_here, NEIGHBORS), jnp.int32),
            pltpu.VMEM((rows_here, NEIGHBORS), f32),
            pltpu.VMEM((nc, piece, cols_here), f32),
            pltpu.VMEM((nc, piece, cols_here), f32),
            pltpu.VMEM((nc, piece, cols_here), f32),
            pltpu.VMEM((rows_here, cols_here), f32),
            pltpu.VMEM((nr, 2 * PIVOT, cols_here), f32),
            pltpu.VMEM((nr, PIVOT, cols_here), f32),
            pltpu.VMEM((2 * PIVOT, cols_here), f32),
            dma((5, 2)),
        ],
        compiler_params=pltpu.CompilerParams(
            collective_id=0, has_side_effects=True, vmem_limit_bytes=60 * 1024 * 1024),
    )(pivots, distances, neighbor_ids, edge_lengths)


def solution(mesh):
    placed = (P("row", "col"), P(), P(None, ("row", "col")), P())
    body = functools.partial(on_device, mesh.shape["row"], mesh.shape["col"])
    return jax.shard_map(
        body, mesh=mesh, in_specs=placed, out_specs=P("row", "col"), check_vma=False
    )
```

```python
import functools

import jax
import jax.numpy as jnp
from jax import lax
from jax.experimental import pallas as pl
from jax.experimental.pallas import tpu as pltpu
from jax.sharding import PartitionSpec as P

NEIGHBORS = 10
PIVOT = 32
MESH = pl.DeviceIdType.MESH


def edge_bound(row_ids, col_ids, ids_rows, len_rows, ids_cols, len_cols):
    bound = jnp.where(row_ids == col_ids, jnp.float32(0.0), jnp.inf)
    for k in range(NEIGHBORS):
        forward = jnp.where(ids_rows[:, k : k + 1] == col_ids, len_rows[:, k : k + 1], jnp.inf)
        backward = jnp.where(row_ids == ids_cols[k : k + 1, :], len_cols[k : k + 1, :], jnp.inf)
        bound = jnp.minimum(bound, jnp.minimum(forward, backward))
    return bound


def minplus(total, left, right):
    for k in range(left.shape[1]):
        term = left[:, k : k + 1] + right[k : k + 1, :]
        total = term if total is None else jnp.minimum(total, term)
    return total


def pick(items, index):
    chosen = items[0]
    index = jnp.full(chosen.shape, index, jnp.int32)
    for i in range(1, len(items)):
        chosen = jnp.where(index == i, items[i], chosen)
    return chosen


def kernel(nr, nc, pivots_in, dist_in, ids_in, lens_in, out, pivots, dist, ids, lens, in_sem,
           e_send, e_all, ids_r, len_r, c_send, c_recv, c_all, c_full, r_recv, k_all, k_ref, t_ref, sems):
    rows_here, cols_here = dist.shape
    width = lens.shape[1]
    depth = e_all.shape[1]
    groups = cols_here // width
    half = rows_here // 2
    piece = half // nc
    pair = 2 * PIVOT
    devices = nr * nc
    r, c = lax.axis_index("row"), lax.axis_index("col")
    me = r * nc + c
    row_peers = [lax.rem(r + i, nr) for i in range(1, nr)]
    col_peers = [lax.rem(c + i, nc) for i in range(1, nc)]

    loads = [
        pltpu.make_async_copy(src, dst, in_sem.at[i])
        for i, (src, dst) in enumerate(
            [(pivots_in, pivots), (dist_in, dist), (lens_in, lens), (ids_in, ids)])
    ]
    for load in loads:
        load.start()

    barrier = pltpu.get_barrier_semaphore()

    def greet(i, carry):
        other = lax.rem(me + i, devices)
        pl.semaphore_signal(barrier, inc=1, device_id=(lax.div(other, nc), lax.rem(other, nc)),
                            device_id_type=MESH)
        return carry

    lax.fori_loop(1, devices, greet, 0)

    for load in loads:
        load.wait()
    p = [pivots[q] for q in range(2)]
    base = [p[q] * PIVOT for q in range(2)]
    row_root = [lax.div(base[q], rows_here) for q in range(2)]
    col_root = [lax.div(base[q], cols_here) for q in range(2)]
    row_slot = [lax.rem(p[q], rows_here // PIVOT) for q in range(2)]
    col_slot = [lax.rem(p[q], cols_here // PIVOT) for q in range(2)]
    row_cuts = [slice(i, i + PIVOT) for i in range(0, rows_here, PIVOT)]

    blocks = cols_here // PIVOT
    lane = lax.broadcasted_iota(jnp.int32, (1, cols_here), 1)
    source = jnp.where(
        lane // PIVOT % 2 == 0, jnp.full_like(lane, col_slot[0]), jnp.full_like(lane, col_slot[1]))
    turn = (lane // PIVOT - source + blocks) % blocks
    packed = jnp.zeros((half, cols_here), jnp.float32)
    for h in range(2):
        part = dist[h * half : (h + 1) * half, :]
        for g in range(blocks):
            turned = pltpu.roll(part, g * PIVOT, 1) if g else part
            packed = jnp.where((turn == g) & (lane // pair == h), turned, packed)
    for j in range(nc):
        c_send[j] = packed[j * piece : (j + 1) * piece, :]
    c_recv[c] = c_send[c]
    own_len = jnp.concatenate(
        [lens[...], jnp.zeros((groups * depth - NEIGHBORS, width), jnp.float32)], axis=0)
    own_len = jnp.concatenate(
        [own_len[g * depth : (g + 1) * depth, :] for g in range(groups)], axis=1)
    own_rows = jnp.concatenate(
        [pick([dist[cut, :] for cut in row_cuts], row_slot[q]) for q in range(2)], axis=0)
    r_recv[r] = own_rows
    own_corner = own_rows
    for g in range(1, blocks):
        turned = pltpu.roll(own_rows, g * PIVOT, 1)
        own_corner = jnp.where((turn == g) & (lane < pair), turned, own_corner)
    last = groups - 1
    levels = pair // depth
    for part in range(pair // width):
        turned = pltpu.roll(own_corner, (last - part) * width % cols_here, 1)
        for m in range(levels):
            e_send[part * levels + m] = jnp.where(
                lane // width == last, turned[m * depth : (m + 1) * depth, :], own_len)
    e_all[me] = e_send[me]

    pl.semaphore_wait(barrier, devices - 1)

    def send(src, dst, kind, peer):
        pltpu.make_async_remote_copy(
            src_ref=src, dst_ref=dst, send_sem=sems.at[kind, 0], recv_sem=sems.at[kind, 1],
            device_id=peer, device_id_type=MESH).start()

    def all_of(buffer, kind):
        count = buffer.shape[0] - 1
        every = buffer.at[pl.ds(0, count)]
        return pltpu.make_async_remote_copy(
            src_ref=every, dst_ref=every, send_sem=sems.at[kind, 0], recv_sem=sems.at[kind, 1],
            device_id=(lax.rem(r + 1, nr), c), device_id_type=MESH)

    def send_edges(i, carry):
        other = lax.rem(me + i, devices)
        send(e_send.at[other], e_all.at[me], 1, (lax.div(other, nc), lax.rem(other, nc)))
        return carry

    lax.fori_loop(1, devices, send_edges, 0)
    for peer in col_peers:
        send(c_send.at[peer], c_recv.at[c], 0, (r, peer))
    for peer in row_peers:
        send(r_recv.at[r], r_recv.at[r], 2, (peer, c))

    for t in range(0, rows_here, cols_here):
        start = pl.multiple_of(r * rows_here + t, cols_here)
        ids_r[t : t + cols_here, :] = ids[:, pl.ds(start, cols_here)].T
    ids_own = ids[:, pl.ds(pl.multiple_of(c * cols_here, cols_here), cols_here)]
    id_tiles = [ids[:, j * cols_here : (j + 1) * cols_here] for j in range(nc)]
    mixed = jnp.zeros_like(ids_own)
    for q in range(2):
        tile = pick(id_tiles, col_root[q])
        for g in range(blocks):
            turned = pltpu.roll(tile, g * PIVOT, 1) if g else tile
            mixed = jnp.where((turn == g) & (lane // PIVOT == q), turned, mixed)
    ids_p = mixed.T[0:pair, :]
    ids_cols = jnp.concatenate([ids_own, mixed], axis=1)
    at_s = lax.broadcasted_iota(jnp.int32, (pair, 1), 0)
    p_rows = jnp.where(at_s < PIVOT, base[0] + at_s, base[1] + at_s - PIVOT)
    p_cols = jnp.where(lane < PIVOT, base[0] + lane, base[1] + lane - PIVOT)
    col_ids = jnp.concatenate([c * cols_here + lane, p_cols], axis=1)

    all_of(e_all, 1).wait_recv()
    everyone = [e_all[i] for i in range(devices)]
    in_first_row = lax.rem(me, levels) * depth < PIVOT
    in_first_col = lax.div(me, levels) * width < PIVOT
    owner = (jnp.where(in_first_row, row_root[0], row_root[1]) * nc
             + jnp.where(in_first_col, col_root[0], col_root[1]))
    mine = pick(everyone, owner)
    flat = jnp.zeros((1, cols_here), jnp.float32)
    for i in range(depth):
        turned = mine[i : i + 1, :]
        if i != last:
            turned = pltpu.roll(turned, (i - last) * width % cols_here, 1)
        flat = jnp.where(lane // width == i, turned, flat)
    k_all[me] = flat

    def send_corner(i, carry):
        other = lax.rem(me + i, devices)
        send(k_all.at[me], k_all.at[me], 4, (lax.div(other, nc), lax.rem(other, nc)))
        return carry

    lax.fori_loop(1, devices, send_corner, 0)
    all_of(c_recv, 0).wait_recv()
    arrived = [c_recv[j] for j in range(nc)]
    c_all[c] = jnp.where(lane % pair < PIVOT, pick(arrived, col_root[0]), pick(arrived, col_root[1]))
    for peer in col_peers:
        send(c_all.at[c], c_all.at[c], 3, (r, peer))

    def spread(tiles):
        parts = []
        for g in range(-(-NEIGHBORS // depth)):
            part = jnp.zeros((depth, cols_here), jnp.float32)
            for i, tile in enumerate(tiles):
                turned = pltpu.roll(tile, (i - g) * width % cols_here, 1) if i != g else tile
                part = jnp.where(lane // width == i, turned, part)
            parts.append(part)
        return jnp.concatenate(parts, axis=0)

    for t in range(0, rows_here, cols_here):
        len_r[t : t + cols_here, :] = spread(
            [e_all[r * nc + t // width + i] for i in range(groups)])[0:NEIGHBORS].T
    len_own = spread([e_all[c * nr + i] for i in range(nr)])
    steps = PIVOT // width
    len_mixed = spread([pick(everyone, p[q] * steps + j) for q in range(2) for j in range(steps)])
    len_p = len_mixed[0:NEIGHBORS].T[0:pair, :]
    len_cols = jnp.concatenate([len_own, len_mixed], axis=1)

    p_bound = edge_bound(p_rows, col_ids, ids_p, len_p, ids_cols, len_cols)
    all_of(r_recv, 2).wait_recv()
    rows_panel = jnp.concatenate(
        [pick([r_recv[i, q * PIVOT : (q + 1) * PIVOT, :] for i in range(nr)], row_root[q])
         for q in range(2)], axis=0)
    rows_panel = jnp.minimum(rows_panel, p_bound[:, 0:cols_here])

    def start_rows(b, carry):
        at = pl.ds(pl.multiple_of(b * PIVOT, PIVOT), PIVOT)
        row_ids = r * rows_here + b * PIVOT + lax.broadcasted_iota(jnp.int32, (PIVOT, 1), 0)
        bound = edge_bound(row_ids, col_ids, ids_r[at, :], len_r[at, :], ids_cols, len_cols)
        out[at, :] = jnp.minimum(dist[at, :], bound[:, 0:cols_here])
        c_full[at, :] = bound[:, cols_here:]
        return carry

    lax.fori_loop(0, rows_here // PIVOT, start_rows, 0)

    all_of(k_all, 4).wait_recv()
    gathered = jnp.concatenate([k_all[i] for i in range(devices)], axis=0)
    for i in range(depth):
        rows = jnp.zeros((levels, cols_here), jnp.float32)
        for part in range(pair // width):
            turned = gathered[part * levels : (part + 1) * levels, :]
            if part != i:
                turned = pltpu.roll(turned, (part - i) * width % cols_here, 1)
            rows = jnp.where(lane // width == part, turned, rows)
        k_ref[pl.ds(i, levels, stride=depth), :] = rows
    corner = k_ref[:, 0:pair]
    corner = jnp.minimum(corner, p_bound[:, cols_here : cols_here + pair])
    corner = lax.fori_loop(0, 6, lambda _, a: minplus(None, a, a), corner)
    t_ref[...] = minplus(None, corner, rows_panel)

    all_of(c_all, 3).wait_recv()
    cols_packed = jnp.concatenate([c_all[j] for j in range(nc)], axis=0)
    c_full[0:half, :] = jnp.minimum(c_full[0:half, :], cols_packed)
    c_full[half:rows_here, :] = jnp.minimum(
        c_full[half:rows_here, :], pltpu.roll(cols_packed, pair, 1))

    def finish(b, carry):
        at = pl.ds(pl.multiple_of(b * PIVOT, PIVOT), PIVOT)
        out[at, :] = minplus(out[at, :], c_full[at, 0:pair], t_ref[...])
        return carry

    lax.fori_loop(0, rows_here // PIVOT, finish, 0)
    for kind, buffer in enumerate([c_recv, e_all, r_recv, c_all, k_all]):
        all_of(buffer, kind).wait_send()


def on_device(nr, nc, distances, neighbor_ids, edge_lengths, pivots):
    rows_here, cols_here = distances.shape
    half = rows_here // 2
    piece = half // nc
    depth = pl.next_power_of_2(pl.cdiv(NEIGHBORS, cols_here // edge_lengths.shape[1]))
    vmem = pl.BlockSpec(memory_space=pltpu.VMEM)
    f32 = jnp.float32
    dma = pltpu.SemaphoreType.DMA
    return pl.pallas_call(
        functools.partial(kernel, nr, nc),
        out_shape=jax.ShapeDtypeStruct(distances.shape, f32),
        in_specs=[pl.BlockSpec(memory_space=pltpu.HBM)] * 4,
        out_specs=vmem,
        scratch_shapes=[
            pltpu.SMEM(pivots.shape, jnp.int32),
            pltpu.VMEM(distances.shape, f32),
            pltpu.VMEM(neighbor_ids.shape, jnp.int32),
            pltpu.VMEM(edge_lengths.shape, f32),
            dma((4,)),
            pltpu.VMEM((nr * nc, depth, cols_here), f32),
            pltpu.VMEM((nr * nc, depth, cols_here), f32),
            pltpu.VMEM((rows_here, NEIGHBORS), jnp.int32),
            pltpu.VMEM((rows_here, NEIGHBORS), f32),
            pltpu.VMEM((nc, piece, cols_here), f32),
            pltpu.VMEM((nc, piece, cols_here), f32),
            pltpu.VMEM((nc, piece, cols_here), f32),
            pltpu.VMEM((rows_here, cols_here), f32),
            pltpu.VMEM((nr, 2 * PIVOT, cols_here), f32),
            pltpu.VMEM((nr * nc, 1, cols_here), f32),
            pltpu.VMEM((2 * PIVOT, cols_here), f32),
            pltpu.VMEM((2 * PIVOT, cols_here), f32),
            dma((5, 2)),
        ],
        compiler_params=pltpu.CompilerParams(
            collective_id=0, has_side_effects=True, vmem_limit_bytes=60 * 1024 * 1024),
    )(pivots, distances, neighbor_ids, edge_lengths)


def solution(mesh):
    placed = (P("row", "col"), P(), P(None, ("row", "col")), P())
    body = functools.partial(on_device, mesh.shape["row"], mesh.shape["col"])
    return jax.shard_map(
        body, mesh=mesh, in_specs=placed, out_specs=P("row", "col"), check_vma=False
    )
```

```python
import functools

import jax
import jax.numpy as jnp
from jax import lax
from jax.experimental import pallas as pl
from jax.experimental.pallas import tpu as pltpu
from jax.sharding import PartitionSpec as P

NEIGHBORS = 10
PIVOT = 32
MESH = pl.DeviceIdType.MESH


def edge_bound(row_ids, col_ids, ids_rows, len_rows, ids_cols, len_cols):
    bound = jnp.where(row_ids == col_ids, jnp.float32(0.0), jnp.inf)
    for k in range(NEIGHBORS):
        forward = jnp.where(ids_rows[:, k : k + 1] == col_ids, len_rows[:, k : k + 1], jnp.inf)
        backward = jnp.where(row_ids == ids_cols[k : k + 1, :], len_cols[k : k + 1, :], jnp.inf)
        bound = jnp.minimum(bound, jnp.minimum(forward, backward))
    return bound


def minplus(total, left, right):
    for k in range(left.shape[1]):
        term = left[:, k : k + 1] + right[k : k + 1, :]
        total = term if total is None else jnp.minimum(total, term)
    return total


def square(twice):
    size = twice.shape[0]
    lane = lax.broadcasted_iota(jnp.int32, twice.shape, 1)
    rows = jnp.where(lane[: size // 2] < size, twice[: size // 2], twice[size // 2 :])
    total = twice
    for k in range(size // 2):
        inner = jnp.where(lane < size, k, k + size // 2)
        left = jnp.take_along_axis(twice, inner, axis=1, mode="promise_in_bounds")
        total = jnp.minimum(total, left + rows[k : k + 1, :])
    return jnp.minimum(total, pltpu.roll(total, size, 1))


def pick(items, index):
    chosen = items[0]
    index = jnp.full(chosen.shape, index, jnp.int32)
    for i in range(1, len(items)):
        chosen = jnp.where(index == i, items[i], chosen)
    return chosen


def kernel(nr, nc, pivots_in, dist_in, ids_in, lens_in, out, pivots, dist, ids, lens, in_sem,
           e_send, e_all, ids_r, len_r, c_send, c_recv, c_all, c_full, r_recv, k_all, k_ref, t_ref, sems):
    rows_here, cols_here = dist.shape
    width = lens.shape[1]
    depth = e_all.shape[1]
    groups = cols_here // width
    half = rows_here // 2
    piece = half // nc
    pair = 2 * PIVOT
    devices = nr * nc
    r, c = lax.axis_index("row"), lax.axis_index("col")
    me = r * nc + c
    row_peers = [lax.rem(r + i, nr) for i in range(1, nr)]
    col_peers = [lax.rem(c + i, nc) for i in range(1, nc)]

    loads = [
        pltpu.make_async_copy(src, dst, in_sem.at[i])
        for i, (src, dst) in enumerate(
            [(pivots_in, pivots), (dist_in, dist), (lens_in, lens), (ids_in, ids)])
    ]
    for load in loads:
        load.start()

    barrier = pltpu.get_barrier_semaphore()

    def greet(i, carry):
        other = lax.rem(me + i, devices)
        pl.semaphore_signal(barrier, inc=1, device_id=(lax.div(other, nc), lax.rem(other, nc)),
                            device_id_type=MESH)
        return carry

    lax.fori_loop(1, devices, greet, 0)

    for load in loads:
        load.wait()
    p = [pivots[q] for q in range(2)]
    base = [p[q] * PIVOT for q in range(2)]
    row_root = [lax.div(base[q], rows_here) for q in range(2)]
    col_root = [lax.div(base[q], cols_here) for q in range(2)]
    row_slot = [lax.rem(p[q], rows_here // PIVOT) for q in range(2)]
    col_slot = [lax.rem(p[q], cols_here // PIVOT) for q in range(2)]
    row_cuts = [slice(i, i + PIVOT) for i in range(0, rows_here, PIVOT)]

    blocks = cols_here // PIVOT
    lane = lax.broadcasted_iota(jnp.int32, (1, cols_here), 1)
    source = jnp.where(
        lane // PIVOT % 2 == 0, jnp.full_like(lane, col_slot[0]), jnp.full_like(lane, col_slot[1]))
    turn = (lane // PIVOT - source + blocks) % blocks
    packed = jnp.zeros((half, cols_here), jnp.float32)
    for h in range(2):
        part = dist[h * half : (h + 1) * half, :]
        for g in range(blocks):
            turned = pltpu.roll(part, g * PIVOT, 1) if g else part
            packed = jnp.where((turn == g) & (lane // pair == h), turned, packed)
    for j in range(nc):
        c_send[j] = packed[j * piece : (j + 1) * piece, :]
    c_recv[c] = c_send[c]
    own_len = jnp.concatenate(
        [lens[...], jnp.zeros((groups * depth - NEIGHBORS, width), jnp.float32)], axis=0)
    own_len = jnp.concatenate(
        [own_len[g * depth : (g + 1) * depth, :] for g in range(groups)], axis=1)
    own_rows = jnp.concatenate(
        [pick([dist[cut, :] for cut in row_cuts], row_slot[q]) for q in range(2)], axis=0)
    r_recv[r] = own_rows
    own_corner = own_rows
    for g in range(1, blocks):
        turned = pltpu.roll(own_rows, g * PIVOT, 1)
        own_corner = jnp.where((turn == g) & (lane < pair), turned, own_corner)
    last = groups - 1
    levels = pair // depth
    for part in range(pair // width):
        turned = pltpu.roll(own_corner, (last - part) * width % cols_here, 1)
        for m in range(levels):
            e_send[part * levels + m] = jnp.where(
                lane // width == last, turned[m * depth : (m + 1) * depth, :], own_len)
    e_all[me] = e_send[me]

    pl.semaphore_wait(barrier, devices - 1)

    def send(src, dst, kind, peer):
        pltpu.make_async_remote_copy(
            src_ref=src, dst_ref=dst, send_sem=sems.at[kind, 0], recv_sem=sems.at[kind, 1],
            device_id=peer, device_id_type=MESH).start()

    def all_of(buffer, kind):
        count = buffer.shape[0] - 1
        every = buffer.at[pl.ds(0, count)]
        return pltpu.make_async_remote_copy(
            src_ref=every, dst_ref=every, send_sem=sems.at[kind, 0], recv_sem=sems.at[kind, 1],
            device_id=(lax.rem(r + 1, nr), c), device_id_type=MESH)

    def send_edges(i, carry):
        other = lax.rem(me + i, devices)
        send(e_send.at[other], e_all.at[me], 1, (lax.div(other, nc), lax.rem(other, nc)))
        return carry

    lax.fori_loop(1, devices, send_edges, 0)
    for peer in col_peers:
        send(c_send.at[peer], c_recv.at[c], 0, (r, peer))
    for peer in row_peers:
        send(r_recv.at[r], r_recv.at[r], 2, (peer, c))

    for t in range(0, rows_here, cols_here):
        start = pl.multiple_of(r * rows_here + t, cols_here)
        ids_r[t : t + cols_here, :] = ids[:, pl.ds(start, cols_here)].T
    ids_own = ids[:, pl.ds(pl.multiple_of(c * cols_here, cols_here), cols_here)]
    id_tiles = [ids[:, j * cols_here : (j + 1) * cols_here] for j in range(nc)]
    mixed = jnp.zeros_like(ids_own)
    for q in range(2):
        tile = pick(id_tiles, col_root[q])
        for g in range(blocks):
            turned = pltpu.roll(tile, g * PIVOT, 1) if g else tile
            mixed = jnp.where((turn == g) & (lane // PIVOT == q), turned, mixed)
    ids_p = mixed.T[0:pair, :]
    ids_cols = jnp.concatenate([ids_own, mixed], axis=1)
    at_s = lax.broadcasted_iota(jnp.int32, (pair, 1), 0)
    p_rows = jnp.where(at_s < PIVOT, base[0] + at_s, base[1] + at_s - PIVOT)
    p_cols = jnp.where(lane < PIVOT, base[0] + lane, base[1] + lane - PIVOT)
    col_ids = jnp.concatenate([c * cols_here + lane, p_cols], axis=1)

    all_of(e_all, 1).wait_recv()
    everyone = [e_all[i] for i in range(devices)]
    in_first_row = lax.rem(me, levels) * depth < PIVOT
    in_first_col = lax.div(me, levels) * width < PIVOT
    owner = (jnp.where(in_first_row, row_root[0], row_root[1]) * nc
             + jnp.where(in_first_col, col_root[0], col_root[1]))
    mine = pick(everyone, owner)
    flat = jnp.zeros((1, cols_here), jnp.float32)
    for i in range(depth):
        turned = mine[i : i + 1, :]
        if i != last:
            turned = pltpu.roll(turned, (i - last) * width % cols_here, 1)
        flat = jnp.where(lane // width == i, turned, flat)
    k_all[me] = flat

    def send_corner(i, carry):
        other = lax.rem(me + i, devices)
        send(k_all.at[me], k_all.at[me], 4, (lax.div(other, nc), lax.rem(other, nc)))
        return carry

    lax.fori_loop(1, devices, send_corner, 0)
    all_of(c_recv, 0).wait_recv()
    arrived = [c_recv[j] for j in range(nc)]
    c_all[c] = jnp.where(lane % pair < PIVOT, pick(arrived, col_root[0]), pick(arrived, col_root[1]))
    for peer in col_peers:
        send(c_all.at[c], c_all.at[c], 3, (r, peer))

    def spread(tiles):
        parts = []
        for g in range(-(-NEIGHBORS // depth)):
            part = jnp.zeros((depth, cols_here), jnp.float32)
            for i, tile in enumerate(tiles):
                turned = pltpu.roll(tile, (i - g) * width % cols_here, 1) if i != g else tile
                part = jnp.where(lane // width == i, turned, part)
            parts.append(part)
        return jnp.concatenate(parts, axis=0)

    for t in range(0, rows_here, cols_here):
        len_r[t : t + cols_here, :] = spread(
            [e_all[r * nc + t // width + i] for i in range(groups)])[0:NEIGHBORS].T
    len_own = spread([e_all[c * nr + i] for i in range(nr)])
    steps = PIVOT // width
    len_mixed = spread([pick(everyone, p[q] * steps + j) for q in range(2) for j in range(steps)])
    len_p = len_mixed[0:NEIGHBORS].T[0:pair, :]
    len_cols = jnp.concatenate([len_own, len_mixed], axis=1)

    p_bound = edge_bound(p_rows, col_ids, ids_p, len_p, ids_cols, len_cols)
    all_of(r_recv, 2).wait_recv()
    rows_panel = jnp.concatenate(
        [pick([r_recv[i, q * PIVOT : (q + 1) * PIVOT, :] for i in range(nr)], row_root[q])
         for q in range(2)], axis=0)
    rows_panel = jnp.minimum(rows_panel, p_bound[:, 0:cols_here])

    def start_rows(b, carry):
        at = pl.ds(pl.multiple_of(b * PIVOT, PIVOT), PIVOT)
        row_ids = r * rows_here + b * PIVOT + lax.broadcasted_iota(jnp.int32, (PIVOT, 1), 0)
        bound = edge_bound(row_ids, col_ids, ids_r[at, :], len_r[at, :], ids_cols, len_cols)
        out[at, :] = jnp.minimum(dist[at, :], bound[:, 0:cols_here])
        c_full[at, :] = bound[:, cols_here:]
        return carry

    lax.fori_loop(0, rows_here // PIVOT, start_rows, 0)

    all_of(k_all, 4).wait_recv()
    gathered = jnp.concatenate([k_all[i] for i in range(devices)], axis=0)
    for i in range(depth):
        rows = jnp.zeros((levels, cols_here), jnp.float32)
        for part in range(pair // width):
            turned = gathered[part * levels : (part + 1) * levels, :]
            if part != i:
                turned = pltpu.roll(turned, (part - i) * width % cols_here, 1)
            rows = jnp.where(lane // width == part, turned, rows)
        k_ref[pl.ds(i, levels, stride=depth), :] = rows
    corner = k_ref[:, 0:pair]
    corner = jnp.minimum(corner, p_bound[:, cols_here : cols_here + pair])
    corner = jnp.concatenate([corner, corner], axis=1)
    corner = lax.fori_loop(0, 6, lambda _, a: square(a), corner)[:, 0:pair]
    t_ref[...] = minplus(None, corner, rows_panel)

    all_of(c_all, 3).wait_recv()
    cols_packed = jnp.concatenate([c_all[j] for j in range(nc)], axis=0)
    c_full[0:half, :] = jnp.minimum(c_full[0:half, :], cols_packed)
    c_full[half:rows_here, :] = jnp.minimum(
        c_full[half:rows_here, :], pltpu.roll(cols_packed, pair, 1))

    def finish(b, carry):
        at = pl.ds(pl.multiple_of(b * PIVOT, PIVOT), PIVOT)
        out[at, :] = minplus(out[at, :], c_full[at, 0:pair], t_ref[...])
        return carry

    lax.fori_loop(0, rows_here // PIVOT, finish, 0)
    for kind, buffer in enumerate([c_recv, e_all, r_recv, c_all, k_all]):
        all_of(buffer, kind).wait_send()


def on_device(nr, nc, distances, neighbor_ids, edge_lengths, pivots):
    rows_here, cols_here = distances.shape
    half = rows_here // 2
    piece = half // nc
    depth = pl.next_power_of_2(pl.cdiv(NEIGHBORS, cols_here // edge_lengths.shape[1]))
    vmem = pl.BlockSpec(memory_space=pltpu.VMEM)
    f32 = jnp.float32
    dma = pltpu.SemaphoreType.DMA
    return pl.pallas_call(
        functools.partial(kernel, nr, nc),
        out_shape=jax.ShapeDtypeStruct(distances.shape, f32),
        in_specs=[pl.BlockSpec(memory_space=pltpu.HBM)] * 4,
        out_specs=vmem,
        scratch_shapes=[
            pltpu.SMEM(pivots.shape, jnp.int32),
            pltpu.VMEM(distances.shape, f32),
            pltpu.VMEM(neighbor_ids.shape, jnp.int32),
            pltpu.VMEM(edge_lengths.shape, f32),
            dma((4,)),
            pltpu.VMEM((nr * nc, depth, cols_here), f32),
            pltpu.VMEM((nr * nc, depth, cols_here), f32),
            pltpu.VMEM((rows_here, NEIGHBORS), jnp.int32),
            pltpu.VMEM((rows_here, NEIGHBORS), f32),
            pltpu.VMEM((nc, piece, cols_here), f32),
            pltpu.VMEM((nc, piece, cols_here), f32),
            pltpu.VMEM((nc, piece, cols_here), f32),
            pltpu.VMEM((rows_here, cols_here), f32),
            pltpu.VMEM((nr, 2 * PIVOT, cols_here), f32),
            pltpu.VMEM((nr * nc, 1, cols_here), f32),
            pltpu.VMEM((2 * PIVOT, cols_here), f32),
            pltpu.VMEM((2 * PIVOT, cols_here), f32),
            dma((5, 2)),
        ],
        compiler_params=pltpu.CompilerParams(
            collective_id=0, has_side_effects=True, vmem_limit_bytes=60 * 1024 * 1024),
    )(pivots, distances, neighbor_ids, edge_lengths)


def solution(mesh):
    placed = (P("row", "col"), P(), P(None, ("row", "col")), P())
    body = functools.partial(on_device, mesh.shape["row"], mesh.shape["col"])
    return jax.shard_map(
        body, mesh=mesh, in_specs=placed, out_specs=P("row", "col"), check_vma=False
    )
```

```python
import functools

import jax
import jax.numpy as jnp
from jax import lax
from jax.experimental import pallas as pl
from jax.experimental.pallas import tpu as pltpu
from jax.sharding import PartitionSpec as P

NEIGHBORS = 10
PIVOT = 32
MESH = pl.DeviceIdType.MESH


def edge_bound(row_ids, col_ids, ids_rows, len_rows, ids_cols, len_cols):
    bound = jnp.where(row_ids == col_ids, jnp.float32(0.0), jnp.inf)
    for k in range(NEIGHBORS):
        forward = jnp.where(ids_rows[:, k : k + 1] == col_ids, len_rows[:, k : k + 1], jnp.inf)
        backward = jnp.where(row_ids == ids_cols[k : k + 1, :], len_cols[k : k + 1, :], jnp.inf)
        bound = jnp.minimum(bound, jnp.minimum(forward, backward))
    return bound


def minplus(total, left, right):
    for k in range(left.shape[1]):
        term = left[:, k : k + 1] + right[k : k + 1, :]
        total = term if total is None else jnp.minimum(total, term)
    return total


def square(twice):
    size = twice.shape[0]
    lane = lax.broadcasted_iota(jnp.int32, twice.shape, 1)
    rows = jnp.where(lane[: size // 2] < size, twice[: size // 2], twice[size // 2 :])
    total = twice
    for k in range(size // 2):
        inner = jnp.where(lane < size, k, k + size // 2)
        left = jnp.take_along_axis(twice, inner, axis=1, mode="promise_in_bounds")
        total = jnp.minimum(total, left + rows[k : k + 1, :])
    return jnp.minimum(total, pltpu.roll(total, size, 1))


def pick(items, index):
    chosen = items[0]
    index = jnp.full(chosen.shape, index, jnp.int32)
    for i in range(1, len(items)):
        chosen = jnp.where(index == i, items[i], chosen)
    return chosen


def kernel(nr, nc, pivots_in, dist_in, ids_in, lens_in, out, pivots, dist, ids, lens, in_sem,
           e_send, e_all, ids_r, len_r, c_send, c_recv, c_all, c_full, r_recv, k_all, k_ref, t_ref, sems):
    rows_here, cols_here = dist.shape
    width = lens.shape[1]
    depth = e_all.shape[1]
    groups = cols_here // width
    half = rows_here // 2
    piece = half // nc
    pair = 2 * PIVOT
    devices = nr * nc
    r, c = lax.axis_index("row"), lax.axis_index("col")
    me = r * nc + c
    row_peers = [lax.rem(r + i, nr) for i in range(1, nr)]
    col_peers = [lax.rem(c + i, nc) for i in range(1, nc)]

    loads = [
        pltpu.make_async_copy(src, dst, in_sem.at[i])
        for i, (src, dst) in enumerate(
            [(pivots_in, pivots), (dist_in, dist), (lens_in, lens), (ids_in, ids)])
    ]
    for load in loads:
        load.start()

    barrier = pltpu.get_barrier_semaphore()

    def every_peer(act):
        if devices > 64:

            def step(i, carry):
                other = lax.rem(me + i, devices)
                act(lax.div(other, nc), lax.rem(other, nc))
                return carry

            lax.fori_loop(1, devices, step, 0)
            return
        for i in range(nr):
            for j in range(nc):
                if i or j:
                    act(row_peers[i - 1] if i else r, col_peers[j - 1] if j else c)

    every_peer(lambda row, col: pl.semaphore_signal(
        barrier, inc=1, device_id=(row, col), device_id_type=MESH))

    for load in loads:
        load.wait()
    p = [pivots[q] for q in range(2)]
    base = [p[q] * PIVOT for q in range(2)]
    row_root = [lax.div(base[q], rows_here) for q in range(2)]
    col_root = [lax.div(base[q], cols_here) for q in range(2)]
    row_slot = [lax.rem(p[q], rows_here // PIVOT) for q in range(2)]
    col_slot = [lax.rem(p[q], cols_here // PIVOT) for q in range(2)]
    row_cuts = [slice(i, i + PIVOT) for i in range(0, rows_here, PIVOT)]

    blocks = cols_here // PIVOT
    lane = lax.broadcasted_iota(jnp.int32, (1, cols_here), 1)
    source = jnp.where(
        lane // PIVOT % 2 == 0, jnp.full_like(lane, col_slot[0]), jnp.full_like(lane, col_slot[1]))
    turn = (lane // PIVOT - source + blocks) % blocks
    packed = jnp.zeros((half, cols_here), jnp.float32)
    for h in range(2):
        part = dist[h * half : (h + 1) * half, :]
        for g in range(blocks):
            turned = pltpu.roll(part, g * PIVOT, 1) if g else part
            packed = jnp.where((turn == g) & (lane // pair == h), turned, packed)
    for j in range(nc):
        c_send[j] = packed[j * piece : (j + 1) * piece, :]
    c_recv[c] = c_send[c]
    own_len = jnp.concatenate(
        [lens[...], jnp.zeros((groups * depth - NEIGHBORS, width), jnp.float32)], axis=0)
    own_len = jnp.concatenate(
        [own_len[g * depth : (g + 1) * depth, :] for g in range(groups)], axis=1)
    own_rows = jnp.concatenate(
        [pick([dist[cut, :] for cut in row_cuts], row_slot[q]) for q in range(2)], axis=0)
    r_recv[r] = own_rows
    own_corner = own_rows
    for g in range(1, blocks):
        turned = pltpu.roll(own_rows, g * PIVOT, 1)
        own_corner = jnp.where((turn == g) & (lane < pair), turned, own_corner)
    last = groups - 1
    levels = pair // depth
    for part in range(pair // width):
        turned = pltpu.roll(own_corner, (last - part) * width % cols_here, 1)
        for m in range(levels):
            e_send[part * levels + m] = jnp.where(
                lane // width == last, turned[m * depth : (m + 1) * depth, :], own_len)
    e_all[me] = e_send[me]

    pl.semaphore_wait(barrier, devices - 1)

    def send(src, dst, kind, peer):
        pltpu.make_async_remote_copy(
            src_ref=src, dst_ref=dst, send_sem=sems.at[kind, 0], recv_sem=sems.at[kind, 1],
            device_id=peer, device_id_type=MESH).start()

    def all_of(buffer, kind):
        count = buffer.shape[0] - 1
        every = buffer.at[pl.ds(0, count)]
        return pltpu.make_async_remote_copy(
            src_ref=every, dst_ref=every, send_sem=sems.at[kind, 0], recv_sem=sems.at[kind, 1],
            device_id=(lax.rem(r + 1, nr), c), device_id_type=MESH)

    every_peer(lambda row, col: send(e_send.at[row * nc + col], e_all.at[me], 1, (row, col)))
    for peer in col_peers:
        send(c_send.at[peer], c_recv.at[c], 0, (r, peer))
    for peer in row_peers:
        send(r_recv.at[r], r_recv.at[r], 2, (peer, c))

    for t in range(0, rows_here, cols_here):
        start = pl.multiple_of(r * rows_here + t, cols_here)
        ids_r[t : t + cols_here, :] = ids[:, pl.ds(start, cols_here)].T
    ids_own = ids[:, pl.ds(pl.multiple_of(c * cols_here, cols_here), cols_here)]
    id_tiles = [ids[:, j * cols_here : (j + 1) * cols_here] for j in range(nc)]
    mixed = jnp.zeros_like(ids_own)
    for q in range(2):
        tile = pick(id_tiles, col_root[q])
        for g in range(blocks):
            turned = pltpu.roll(tile, g * PIVOT, 1) if g else tile
            mixed = jnp.where((turn == g) & (lane // PIVOT == q), turned, mixed)
    ids_p = mixed.T[0:pair, :]
    ids_cols = jnp.concatenate([ids_own, mixed], axis=1)
    at_s = lax.broadcasted_iota(jnp.int32, (pair, 1), 0)
    p_rows = jnp.where(at_s < PIVOT, base[0] + at_s, base[1] + at_s - PIVOT)
    p_cols = jnp.where(lane < PIVOT, base[0] + lane, base[1] + lane - PIVOT)
    col_ids = jnp.concatenate([c * cols_here + lane, p_cols], axis=1)

    all_of(e_all, 1).wait_recv()
    everyone = [e_all[i] for i in range(devices)]
    in_first_row = lax.rem(me, levels) * depth < PIVOT
    in_first_col = lax.div(me, levels) * width < PIVOT
    owner = (jnp.where(in_first_row, row_root[0], row_root[1]) * nc
             + jnp.where(in_first_col, col_root[0], col_root[1]))
    mine = pick(everyone, owner)
    flat = jnp.zeros((1, cols_here), jnp.float32)
    for i in range(depth):
        turned = mine[i : i + 1, :]
        if i != last:
            turned = pltpu.roll(turned, (i - last) * width % cols_here, 1)
        flat = jnp.where(lane // width == i, turned, flat)
    k_all[me] = flat

    every_peer(lambda row, col: send(k_all.at[me], k_all.at[me], 4, (row, col)))
    all_of(c_recv, 0).wait_recv()
    arrived = [c_recv[j] for j in range(nc)]
    c_all[c] = jnp.where(lane % pair < PIVOT, pick(arrived, col_root[0]), pick(arrived, col_root[1]))
    for peer in col_peers:
        send(c_all.at[c], c_all.at[c], 3, (r, peer))

    def spread(tiles):
        parts = []
        for g in range(-(-NEIGHBORS // depth)):
            part = jnp.zeros((depth, cols_here), jnp.float32)
            for i, tile in enumerate(tiles):
                turned = pltpu.roll(tile, (i - g) * width % cols_here, 1) if i != g else tile
                part = jnp.where(lane // width == i, turned, part)
            parts.append(part)
        return jnp.concatenate(parts, axis=0)

    for t in range(0, rows_here, cols_here):
        len_r[t : t + cols_here, :] = spread(
            [e_all[r * nc + t // width + i] for i in range(groups)])[0:NEIGHBORS].T
    len_own = spread([e_all[c * nr + i] for i in range(nr)])
    steps = PIVOT // width
    len_mixed = spread([pick(everyone, p[q] * steps + j) for q in range(2) for j in range(steps)])
    len_p = len_mixed[0:NEIGHBORS].T[0:pair, :]
    len_cols = jnp.concatenate([len_own, len_mixed], axis=1)

    p_bound = edge_bound(p_rows, col_ids, ids_p, len_p, ids_cols, len_cols)
    all_of(r_recv, 2).wait_recv()
    rows_panel = jnp.concatenate(
        [pick([r_recv[i, q * PIVOT : (q + 1) * PIVOT, :] for i in range(nr)], row_root[q])
         for q in range(2)], axis=0)
    rows_panel = jnp.minimum(rows_panel, p_bound[:, 0:cols_here])

    def start_rows(b, carry):
        at = pl.ds(pl.multiple_of(b * PIVOT, PIVOT), PIVOT)
        row_ids = r * rows_here + b * PIVOT + lax.broadcasted_iota(jnp.int32, (PIVOT, 1), 0)
        bound = edge_bound(row_ids, col_ids, ids_r[at, :], len_r[at, :], ids_cols, len_cols)
        out[at, :] = jnp.minimum(dist[at, :], bound[:, 0:cols_here])
        c_full[at, :] = bound[:, cols_here:]
        return carry

    lax.fori_loop(0, rows_here // PIVOT, start_rows, 0)

    all_of(k_all, 4).wait_recv()
    gathered = jnp.concatenate([k_all[i] for i in range(devices)], axis=0)
    for i in range(depth):
        rows = jnp.zeros((levels, cols_here), jnp.float32)
        for part in range(pair // width):
            turned = gathered[part * levels : (part + 1) * levels, :]
            if part != i:
                turned = pltpu.roll(turned, (part - i) * width % cols_here, 1)
            rows = jnp.where(lane // width == part, turned, rows)
        k_ref[pl.ds(i, levels, stride=depth), :] = rows
    corner = k_ref[:, 0:pair]
    corner = jnp.minimum(corner, p_bound[:, cols_here : cols_here + pair])
    corner = jnp.concatenate([corner, corner], axis=1)
    corner = lax.fori_loop(0, 6, lambda _, a: square(a), corner)[:, 0:pair]
    t_ref[...] = minplus(None, corner, rows_panel)

    all_of(c_all, 3).wait_recv()
    cols_packed = jnp.concatenate([c_all[j] for j in range(nc)], axis=0)
    c_full[0:half, :] = jnp.minimum(c_full[0:half, :], cols_packed)
    c_full[half:rows_here, :] = jnp.minimum(
        c_full[half:rows_here, :], pltpu.roll(cols_packed, pair, 1))

    def finish(b, carry):
        at = pl.ds(pl.multiple_of(b * PIVOT, PIVOT), PIVOT)
        out[at, :] = minplus(out[at, :], c_full[at, 0:pair], t_ref[...])
        return carry

    lax.fori_loop(0, rows_here // PIVOT, finish, 0)
    for kind, buffer in enumerate([c_recv, e_all, r_recv, c_all, k_all]):
        all_of(buffer, kind).wait_send()


def on_device(nr, nc, distances, neighbor_ids, edge_lengths, pivots):
    rows_here, cols_here = distances.shape
    half = rows_here // 2
    piece = half // nc
    depth = pl.next_power_of_2(pl.cdiv(NEIGHBORS, cols_here // edge_lengths.shape[1]))
    vmem = pl.BlockSpec(memory_space=pltpu.VMEM)
    f32 = jnp.float32
    dma = pltpu.SemaphoreType.DMA
    return pl.pallas_call(
        functools.partial(kernel, nr, nc),
        out_shape=jax.ShapeDtypeStruct(distances.shape, f32),
        in_specs=[pl.BlockSpec(memory_space=pltpu.HBM)] * 4,
        out_specs=vmem,
        scratch_shapes=[
            pltpu.SMEM(pivots.shape, jnp.int32),
            pltpu.VMEM(distances.shape, f32),
            pltpu.VMEM(neighbor_ids.shape, jnp.int32),
            pltpu.VMEM(edge_lengths.shape, f32),
            dma((4,)),
            pltpu.VMEM((nr * nc, depth, cols_here), f32),
            pltpu.VMEM((nr * nc, depth, cols_here), f32),
            pltpu.VMEM((rows_here, NEIGHBORS), jnp.int32),
            pltpu.VMEM((rows_here, NEIGHBORS), f32),
            pltpu.VMEM((nc, piece, cols_here), f32),
            pltpu.VMEM((nc, piece, cols_here), f32),
            pltpu.VMEM((nc, piece, cols_here), f32),
            pltpu.VMEM((rows_here, cols_here), f32),
            pltpu.VMEM((nr, 2 * PIVOT, cols_here), f32),
            pltpu.VMEM((nr * nc, 1, cols_here), f32),
            pltpu.VMEM((2 * PIVOT, cols_here), f32),
            pltpu.VMEM((2 * PIVOT, cols_here), f32),
            dma((5, 2)),
        ],
        compiler_params=pltpu.CompilerParams(
            collective_id=0, has_side_effects=True, vmem_limit_bytes=32 * 1024 * 1024),
    )(*[pltpu.with_memory_space_constraint(x, pltpu.HBM)
        for x in (pivots, distances, neighbor_ids, edge_lengths)])


def solution(mesh):
    placed = (P("row", "col"), P(), P(None, ("row", "col")), P())
    body = functools.partial(on_device, mesh.shape["row"], mesh.shape["col"])
    return jax.shard_map(
        body, mesh=mesh, in_specs=placed, out_specs=P("row", "col"), check_vma=False
    )
```

```python
import functools

import jax
import jax.numpy as jnp
from jax import lax
from jax.experimental import pallas as pl
from jax.experimental.pallas import tpu as pltpu
from jax.sharding import PartitionSpec as P

NEIGHBORS = 10
PIVOT = 32
MESH = pl.DeviceIdType.MESH


def edge_bound(row_ids, col_ids, ids_rows, len_rows, ids_cols, len_cols):
    bound = jnp.where(row_ids == col_ids, jnp.float32(0.0), jnp.inf)
    for k in range(NEIGHBORS):
        forward = jnp.where(ids_rows[:, k : k + 1] == col_ids, len_rows[:, k : k + 1], jnp.inf)
        backward = jnp.where(row_ids == ids_cols[k : k + 1, :], len_cols[k : k + 1, :], jnp.inf)
        bound = jnp.minimum(bound, jnp.minimum(forward, backward))
    return bound


def minplus(total, left, right):
    for k in range(left.shape[1]):
        term = left[:, k : k + 1] + right[k : k + 1, :]
        total = term if total is None else jnp.minimum(total, term)
    return total


def square(twice, rows_ref):
    size = twice.shape[0]
    lane = lax.broadcasted_iota(jnp.int32, twice.shape, 1)
    rows_ref[...] = jnp.where(lane[: size // 2] < size, twice[: size // 2], twice[size // 2 :])
    total = twice
    for k in range(size // 2):
        inner = jnp.where(lane < size, k, k + size // 2)
        left = jnp.take_along_axis(twice, inner, axis=1, mode="promise_in_bounds")
        total = jnp.minimum(total, left + rows_ref[k : k + 1, :])
    return jnp.minimum(total, pltpu.roll(total, size, 1))


def pick(items, index):
    chosen = items[0]
    index = jnp.full(chosen.shape, index, jnp.int32)
    for i in range(1, len(items)):
        chosen = jnp.where(index == i, items[i], chosen)
    return chosen


def kernel(nr, nc, pivots_in, dist_in, ids_in, lens_in, out, pivots, dist, ids, lens, in_sem,
           e_send, e_all, ids_r, len_r, c_send, c_recv, c_all, c_full, r_recv, k_all, k_ref, t_ref, sems):
    rows_here, cols_here = dist.shape
    width = lens.shape[1]
    depth = e_all.shape[1]
    groups = cols_here // width
    half = rows_here // 2
    piece = half // nc
    pair = 2 * PIVOT
    devices = nr * nc
    r, c = lax.axis_index("row"), lax.axis_index("col")
    me = r * nc + c
    row_peers = [lax.rem(r + i, nr) for i in range(1, nr)]
    col_peers = [lax.rem(c + i, nc) for i in range(1, nc)]

    loads = [
        pltpu.make_async_copy(src, dst, in_sem.at[i])
        for i, (src, dst) in enumerate(
            [(pivots_in, pivots), (dist_in, dist), (lens_in, lens), (ids_in, ids)])
    ]
    for load in loads:
        load.start()

    barrier = pltpu.get_barrier_semaphore()

    def every_peer(act):
        if devices > 64:

            def step(i, carry):
                other = lax.rem(me + i, devices)
                act(lax.div(other, nc), lax.rem(other, nc))
                return carry

            lax.fori_loop(1, devices, step, 0)
            return
        for i in range(nr):
            for j in range(nc):
                if i or j:
                    act(row_peers[i - 1] if i else r, col_peers[j - 1] if j else c)

    every_peer(lambda row, col: pl.semaphore_signal(
        barrier, inc=1, device_id=(row, col), device_id_type=MESH))

    for load in loads:
        load.wait()
    p = [pivots[q] for q in range(2)]
    base = [p[q] * PIVOT for q in range(2)]
    row_root = [lax.div(base[q], rows_here) for q in range(2)]
    col_root = [lax.div(base[q], cols_here) for q in range(2)]
    row_slot = [lax.rem(p[q], rows_here // PIVOT) for q in range(2)]
    col_slot = [lax.rem(p[q], cols_here // PIVOT) for q in range(2)]
    row_cuts = [slice(i, i + PIVOT) for i in range(0, rows_here, PIVOT)]

    blocks = cols_here // PIVOT
    lane = lax.broadcasted_iota(jnp.int32, (1, cols_here), 1)
    source = jnp.where(
        lane // PIVOT % 2 == 0, jnp.full_like(lane, col_slot[0]), jnp.full_like(lane, col_slot[1]))
    turn = (lane // PIVOT - source + blocks) % blocks
    own_len = jnp.concatenate(
        [lens[...], jnp.zeros((groups * depth - NEIGHBORS, width), jnp.float32)], axis=0)
    own_len = jnp.concatenate(
        [own_len[g * depth : (g + 1) * depth, :] for g in range(groups)], axis=1)
    own_rows = jnp.concatenate(
        [pick([dist[cut, :] for cut in row_cuts], row_slot[q]) for q in range(2)], axis=0)
    r_recv[r] = own_rows
    own_corner = own_rows
    for g in range(1, blocks):
        turned = pltpu.roll(own_rows, g * PIVOT, 1)
        own_corner = jnp.where((turn == g) & (lane < pair), turned, own_corner)
    last = groups - 1
    levels = pair // depth
    for part in range(pair // width):
        turned = pltpu.roll(own_corner, (last - part) * width % cols_here, 1)
        for m in range(levels):
            e_send[part * levels + m] = jnp.where(
                lane // width == last, turned[m * depth : (m + 1) * depth, :], own_len)
    e_all[me] = e_send[me]

    pl.semaphore_wait(barrier, devices - 1)

    def send(src, dst, kind, peer):
        pltpu.make_async_remote_copy(
            src_ref=src, dst_ref=dst, send_sem=sems.at[kind, 0], recv_sem=sems.at[kind, 1],
            device_id=peer, device_id_type=MESH).start()

    def all_of(buffer, kind):
        count = buffer.shape[0] - 1
        every = buffer.at[pl.ds(0, count)]
        return pltpu.make_async_remote_copy(
            src_ref=every, dst_ref=every, send_sem=sems.at[kind, 0], recv_sem=sems.at[kind, 1],
            device_id=(lax.rem(r + 1, nr), c), device_id_type=MESH)

    every_peer(lambda row, col: send(e_send.at[row * nc + col], e_all.at[me], 1, (row, col)))
    packed = jnp.zeros((half, cols_here), jnp.float32)
    for h in range(2):
        part = dist[h * half : (h + 1) * half, :]
        for g in range(blocks):
            turned = pltpu.roll(part, g * PIVOT, 1) if g else part
            packed = jnp.where((turn == g) & (lane // pair == h), turned, packed)
    for j in range(nc):
        c_send[j] = packed[j * piece : (j + 1) * piece, :]
    c_recv[c] = c_send[c]
    for peer in col_peers:
        send(c_send.at[peer], c_recv.at[c], 0, (r, peer))
    for peer in row_peers:
        send(r_recv.at[r], r_recv.at[r], 2, (peer, c))

    for t in range(0, rows_here, cols_here):
        start = pl.multiple_of(r * rows_here + t, cols_here)
        ids_r[t : t + cols_here, :] = ids[:, pl.ds(start, cols_here)].T
    ids_own = ids[:, pl.ds(pl.multiple_of(c * cols_here, cols_here), cols_here)]
    id_tiles = [ids[:, j * cols_here : (j + 1) * cols_here] for j in range(nc)]
    mixed = jnp.zeros_like(ids_own)
    for q in range(2):
        tile = pick(id_tiles, col_root[q])
        for g in range(blocks):
            turned = pltpu.roll(tile, g * PIVOT, 1) if g else tile
            mixed = jnp.where((turn == g) & (lane // PIVOT == q), turned, mixed)
    ids_p = mixed.T[0:pair, :]
    ids_cols = jnp.concatenate([ids_own, mixed], axis=1)
    at_s = lax.broadcasted_iota(jnp.int32, (pair, 1), 0)
    p_rows = jnp.where(at_s < PIVOT, base[0] + at_s, base[1] + at_s - PIVOT)
    p_cols = jnp.where(lane < PIVOT, base[0] + lane, base[1] + lane - PIVOT)
    col_ids = jnp.concatenate([c * cols_here + lane, p_cols], axis=1)

    all_of(e_all, 1).wait_recv()
    everyone = [e_all[i] for i in range(devices)]
    in_first_row = lax.rem(me, levels) * depth < PIVOT
    in_first_col = lax.div(me, levels) * width < PIVOT
    owner = (jnp.where(in_first_row, row_root[0], row_root[1]) * nc
             + jnp.where(in_first_col, col_root[0], col_root[1]))
    mine = pick(everyone, owner)
    flat = jnp.zeros((1, cols_here), jnp.float32)
    for i in range(depth):
        turned = mine[i : i + 1, :]
        if i != last:
            turned = pltpu.roll(turned, (i - last) * width % cols_here, 1)
        flat = jnp.where(lane // width == i, turned, flat)
    k_all[me] = flat

    every_peer(lambda row, col: send(k_all.at[me], k_all.at[me], 4, (row, col)))
    all_of(c_recv, 0).wait_recv()
    arrived = [c_recv[j] for j in range(nc)]
    c_all[c] = jnp.where(lane % pair < PIVOT, pick(arrived, col_root[0]), pick(arrived, col_root[1]))
    for peer in col_peers:
        send(c_all.at[c], c_all.at[c], 3, (r, peer))

    def spread(tiles):
        parts = []
        for g in range(-(-NEIGHBORS // depth)):
            part = jnp.zeros((depth, cols_here), jnp.float32)
            for i, tile in enumerate(tiles):
                turned = pltpu.roll(tile, (i - g) * width % cols_here, 1) if i != g else tile
                part = jnp.where(lane // width == i, turned, part)
            parts.append(part)
        return jnp.concatenate(parts, axis=0)

    for t in range(0, rows_here, cols_here):
        len_r[t : t + cols_here, :] = spread(
            [e_all[r * nc + t // width + i] for i in range(groups)])[0:NEIGHBORS].T
    len_own = spread([e_all[c * nr + i] for i in range(nr)])
    steps = PIVOT // width
    len_mixed = spread([pick(everyone, p[q] * steps + j) for q in range(2) for j in range(steps)])
    len_p = len_mixed[0:NEIGHBORS].T[0:pair, :]
    len_cols = jnp.concatenate([len_own, len_mixed], axis=1)

    p_bound = edge_bound(p_rows, col_ids, ids_p, len_p, ids_cols, len_cols)
    all_of(r_recv, 2).wait_recv()
    rows_panel = jnp.concatenate(
        [pick([r_recv[i, q * PIVOT : (q + 1) * PIVOT, :] for i in range(nr)], row_root[q])
         for q in range(2)], axis=0)
    rows_panel = jnp.minimum(rows_panel, p_bound[:, 0:cols_here])

    def start_rows(b, carry):
        at = pl.ds(pl.multiple_of(b * PIVOT, PIVOT), PIVOT)
        row_ids = r * rows_here + b * PIVOT + lax.broadcasted_iota(jnp.int32, (PIVOT, 1), 0)
        bound = edge_bound(row_ids, col_ids, ids_r[at, :], len_r[at, :], ids_cols, len_cols)
        out[at, :] = jnp.minimum(dist[at, :], bound[:, 0:cols_here])
        c_full[at, :] = bound[:, cols_here:]
        return carry

    lax.fori_loop(0, rows_here // PIVOT, start_rows, 0)

    all_of(k_all, 4).wait_recv()
    gathered = jnp.concatenate([k_all[i] for i in range(devices)], axis=0)
    for i in range(depth):
        rows = jnp.zeros((levels, cols_here), jnp.float32)
        for part in range(pair // width):
            turned = gathered[part * levels : (part + 1) * levels, :]
            if part != i:
                turned = pltpu.roll(turned, (part - i) * width % cols_here, 1)
            rows = jnp.where(lane // width == part, turned, rows)
        k_ref[pl.ds(i, levels, stride=depth), :] = rows
    corner = k_ref[:, 0:pair]
    corner = jnp.minimum(corner, p_bound[:, cols_here : cols_here + pair])
    corner = jnp.concatenate([corner, corner], axis=1)
    corner = lax.fori_loop(0, 6, lambda _, a: square(a, t_ref.at[0:PIVOT, :]), corner)[:, 0:pair]
    k_ref[...] = rows_panel
    t_ref[...] = minplus(None, corner, k_ref)

    all_of(c_all, 3).wait_recv()
    cols_packed = jnp.concatenate([c_all[j] for j in range(nc)], axis=0)
    c_full[0:half, :] = jnp.minimum(c_full[0:half, :], cols_packed)
    c_full[half:rows_here, :] = jnp.minimum(
        c_full[half:rows_here, :], pltpu.roll(cols_packed, pair, 1))

    def finish(b, carry):
        at = pl.ds(pl.multiple_of(b * PIVOT, PIVOT), PIVOT)
        out[at, :] = minplus(out[at, :], c_full[at, 0:pair], t_ref)
        return carry

    lax.fori_loop(0, rows_here // PIVOT, finish, 0)
    for kind, buffer in enumerate([c_recv, e_all, r_recv, c_all, k_all]):
        all_of(buffer, kind).wait_send()


def on_device(nr, nc, distances, neighbor_ids, edge_lengths, pivots):
    rows_here, cols_here = distances.shape
    half = rows_here // 2
    piece = half // nc
    depth = pl.next_power_of_2(pl.cdiv(NEIGHBORS, cols_here // edge_lengths.shape[1]))
    vmem = pl.BlockSpec(memory_space=pltpu.VMEM)
    f32 = jnp.float32
    dma = pltpu.SemaphoreType.DMA
    return pl.pallas_call(
        functools.partial(kernel, nr, nc),
        out_shape=jax.ShapeDtypeStruct(distances.shape, f32),
        in_specs=[pl.BlockSpec(memory_space=pltpu.HBM)] * 4,
        out_specs=vmem,
        scratch_shapes=[
            pltpu.SMEM(pivots.shape, jnp.int32),
            pltpu.VMEM(distances.shape, f32),
            pltpu.VMEM(neighbor_ids.shape, jnp.int32),
            pltpu.VMEM(edge_lengths.shape, f32),
            dma((4,)),
            pltpu.VMEM((nr * nc, depth, cols_here), f32),
            pltpu.VMEM((nr * nc, depth, cols_here), f32),
            pltpu.VMEM((rows_here, NEIGHBORS), jnp.int32),
            pltpu.VMEM((rows_here, NEIGHBORS), f32),
            pltpu.VMEM((nc, piece, cols_here), f32),
            pltpu.VMEM((nc, piece, cols_here), f32),
            pltpu.VMEM((nc, piece, cols_here), f32),
            pltpu.VMEM((rows_here, cols_here), f32),
            pltpu.VMEM((nr, 2 * PIVOT, cols_here), f32),
            pltpu.VMEM((nr * nc, 1, cols_here), f32),
            pltpu.VMEM((2 * PIVOT, cols_here), f32),
            pltpu.VMEM((2 * PIVOT, cols_here), f32),
            dma((5, 2)),
        ],
        compiler_params=pltpu.CompilerParams(
            collective_id=0, has_side_effects=True, vmem_limit_bytes=32 * 1024 * 1024),
    )(*[pltpu.with_memory_space_constraint(x, pltpu.HBM)
        for x in (pivots, distances, neighbor_ids, edge_lengths)])


def solution(mesh):
    placed = (P("row", "col"), P(), P(None, ("row", "col")), P())
    body = functools.partial(on_device, mesh.shape["row"], mesh.shape["col"])
    return jax.shard_map(
        body, mesh=mesh, in_specs=placed, out_specs=P("row", "col"), check_vma=False
    )
```

```python
import functools

import jax
import jax.numpy as jnp
from jax import lax
from jax.experimental import pallas as pl
from jax.experimental.pallas import tpu as pltpu
from jax.sharding import PartitionSpec as P

NEIGHBORS = 10
PIVOT = 32
MESH = pl.DeviceIdType.MESH


def edge_bound(row_ids, col_ids, ids_rows, len_rows, ids_cols, len_cols):
    bound = jnp.where(row_ids == col_ids, jnp.float32(0.0), jnp.inf)
    for k in range(NEIGHBORS):
        forward = jnp.where(ids_rows[:, k : k + 1] == col_ids, len_rows[:, k : k + 1], jnp.inf)
        backward = jnp.where(row_ids == ids_cols[k : k + 1, :], len_cols[k : k + 1, :], jnp.inf)
        bound = jnp.minimum(bound, jnp.minimum(forward, backward))
    return bound


def square(twice, rows_ref):
    size = twice.shape[0]
    lane = lax.broadcasted_iota(jnp.int32, twice.shape, 1)
    rows_ref[...] = jnp.where(lane[: size // 2] < size, twice[: size // 2], twice[size // 2 :])
    total = twice
    for k in range(size // 2):
        inner = jnp.where(lane < size, k, k + size // 2)
        left = jnp.take_along_axis(twice, inner, axis=1, mode="promise_in_bounds")
        total = jnp.minimum(total, left + rows_ref[k : k + 1, :])
    return jnp.minimum(total, pltpu.roll(total, size, 1))


def pick(items, index):
    chosen = items[0]
    index = jnp.full(chosen.shape, index, jnp.int32)
    for i in range(1, len(items)):
        chosen = jnp.where(index == i, items[i], chosen)
    return chosen


def kernel(nr, nc, pivots_in, dist_in, ids_in, lens_in, out, pivots, dist, ids, lens, in_sem,
           e_send, e_all, ids_r, len_r, c_send, c_recv, c_all, left, r_recv, k_all, k_ref, work, id_ref, bounds, sems):
    rows_here, cols_here = dist.shape
    width = lens.shape[1]
    depth = e_all.shape[1]
    groups = cols_here // width
    half = rows_here // 2
    piece = half // nc
    pair = 2 * PIVOT
    devices = nr * nc
    r, c = lax.axis_index("row"), lax.axis_index("col")
    me = r * nc + c
    row_peers = [lax.rem(r + i, nr) for i in range(1, nr)]
    col_peers = [lax.rem(c + i, nc) for i in range(1, nc)]

    loads = [
        pltpu.make_async_copy(src, dst, in_sem.at[i])
        for i, (src, dst) in enumerate(
            [(pivots_in, pivots), (dist_in, dist), (lens_in, lens), (ids_in, ids)])
    ]
    for load in loads:
        load.start()

    barrier = pltpu.get_barrier_semaphore()

    def every_peer(act):
        if devices > 1:

            def step(i, carry):
                other = lax.rem(me + i, devices)
                act(lax.div(other, nc), lax.rem(other, nc))
                return carry

            lax.fori_loop(1, devices, step, 0)
            return
        for i in range(nr):
            for j in range(nc):
                if i or j:
                    act(row_peers[i - 1] if i else r, col_peers[j - 1] if j else c)

    every_peer(lambda row, col: pl.semaphore_signal(
        barrier, inc=1, device_id=(row, col), device_id_type=MESH))

    for load in loads:
        load.wait()
    p = [pivots[q] for q in range(2)]
    base = [p[q] * PIVOT for q in range(2)]
    row_root = [lax.div(base[q], rows_here) for q in range(2)]
    col_root = [lax.div(base[q], cols_here) for q in range(2)]
    row_slot = [lax.rem(p[q], rows_here // PIVOT) for q in range(2)]
    col_slot = [lax.rem(p[q], cols_here // PIVOT) for q in range(2)]
    row_cuts = [slice(i, i + PIVOT) for i in range(0, rows_here, PIVOT)]

    blocks = cols_here // PIVOT
    lane = lax.broadcasted_iota(jnp.int32, (1, cols_here), 1)
    source = jnp.where(
        lane // PIVOT % 2 == 0, jnp.full_like(lane, col_slot[0]), jnp.full_like(lane, col_slot[1]))
    turn = (lane // PIVOT - source + blocks) % blocks
    own_len = jnp.concatenate(
        [lens[...], jnp.zeros((groups * depth - NEIGHBORS, width), jnp.float32)], axis=0)
    own_len = jnp.concatenate(
        [own_len[g * depth : (g + 1) * depth, :] for g in range(groups)], axis=1)
    own_rows = jnp.concatenate(
        [pick([dist[cut, :] for cut in row_cuts], row_slot[q]) for q in range(2)], axis=0)
    r_recv[r] = own_rows
    own_corner = own_rows
    for g in range(1, blocks):
        turned = pltpu.roll(own_rows, g * PIVOT, 1)
        own_corner = jnp.where((turn == g) & (lane < pair), turned, own_corner)
    last = groups - 1
    levels = pair // depth
    for part in range(pair // width):
        turned = pltpu.roll(own_corner, (last - part) * width % cols_here, 1)
        for m in range(levels):
            e_send[part * levels + m] = jnp.where(
                lane // width == last, turned[m * depth : (m + 1) * depth, :], own_len)
    e_all[me] = e_send[me]

    pl.semaphore_wait(barrier, devices - 1)

    def send(src, dst, kind, peer):
        pltpu.make_async_remote_copy(
            src_ref=src, dst_ref=dst, send_sem=sems.at[kind, 0], recv_sem=sems.at[kind, 1],
            device_id=peer, device_id_type=MESH).start()

    def all_of(buffer, kind):
        count = buffer.shape[0] - 1
        every = buffer.at[pl.ds(0, count)]
        return pltpu.make_async_remote_copy(
            src_ref=every, dst_ref=every, send_sem=sems.at[kind, 0], recv_sem=sems.at[kind, 1],
            device_id=(lax.rem(r + 1, nr), c), device_id_type=MESH)

    every_peer(lambda row, col: send(e_send.at[row * nc + col], e_all.at[me], 1, (row, col)))
    packed = jnp.zeros((half, cols_here), jnp.float32)
    for h in range(2):
        part = dist[h * half : (h + 1) * half, :]
        for g in range(blocks):
            turned = pltpu.roll(part, g * PIVOT, 1) if g else part
            packed = jnp.where((turn == g) & (lane // pair == h), turned, packed)
    for j in range(nc):
        c_send[j] = packed[j * piece : (j + 1) * piece, :]
    c_recv[c] = c_send[c]
    for peer in col_peers:
        send(c_send.at[peer], c_recv.at[c], 0, (r, peer))
    for peer in row_peers:
        send(r_recv.at[r], r_recv.at[r], 2, (peer, c))

    for t in range(0, rows_here, cols_here):
        start = pl.multiple_of(r * rows_here + t, cols_here)
        ids_r[pair + t : pair + t + cols_here, :] = ids[:, pl.ds(start, cols_here)].T
    ids_own = ids[:, pl.ds(pl.multiple_of(c * cols_here, cols_here), cols_here)]
    id_tiles = [ids[:, j * cols_here : (j + 1) * cols_here] for j in range(nc)]
    mixed = jnp.zeros_like(ids_own)
    for q in range(2):
        tile = pick(id_tiles, col_root[q])
        for g in range(blocks):
            turned = pltpu.roll(tile, g * PIVOT, 1) if g else tile
            mixed = jnp.where((turn == g) & (lane // PIVOT == q), turned, mixed)
    ids_r[0:pair, :] = mixed.T[0:pair, :]
    ids_cols = jnp.concatenate([ids_own, mixed], axis=1)
    at_s = lax.broadcasted_iota(jnp.int32, (pair, 1), 0)
    id_ref[0:pair, :] = jnp.where(at_s < PIVOT, base[0] + at_s, base[1] + at_s - PIVOT)
    id_ref[pair:, :] = r * rows_here + lax.broadcasted_iota(jnp.int32, (rows_here, 1), 0)
    p_cols = jnp.where(lane < PIVOT, base[0] + lane, base[1] + lane - PIVOT)
    col_ids = jnp.concatenate([c * cols_here + lane, p_cols], axis=1)

    all_of(e_all, 1).wait_recv()
    everyone = [e_all[i] for i in range(devices)]
    in_first_row = lax.rem(me, levels) * depth < PIVOT
    in_first_col = lax.div(me, levels) * width < PIVOT
    owner = (jnp.where(in_first_row, row_root[0], row_root[1]) * nc
             + jnp.where(in_first_col, col_root[0], col_root[1]))
    mine = pick(everyone, owner)
    flat = jnp.zeros((1, cols_here), jnp.float32)
    for i in range(depth):
        turned = mine[i : i + 1, :]
        if i != last:
            turned = pltpu.roll(turned, (i - last) * width % cols_here, 1)
        flat = jnp.where(lane // width == i, turned, flat)
    k_all[me] = flat

    every_peer(lambda row, col: send(k_all.at[me], k_all.at[me], 4, (row, col)))
    all_of(c_recv, 0).wait_recv()
    arrived = [c_recv[j] for j in range(nc)]
    c_all[c] = jnp.where(lane % pair < PIVOT, pick(arrived, col_root[0]), pick(arrived, col_root[1]))
    for peer in col_peers:
        send(c_all.at[c], c_all.at[c], 3, (r, peer))

    def spread(tiles):
        parts = []
        for g in range(-(-NEIGHBORS // depth)):
            part = jnp.zeros((depth, cols_here), jnp.float32)
            for i, tile in enumerate(tiles):
                turned = pltpu.roll(tile, (i - g) * width % cols_here, 1) if i != g else tile
                part = jnp.where(lane // width == i, turned, part)
            parts.append(part)
        return jnp.concatenate(parts, axis=0)

    for t in range(0, rows_here, cols_here):
        len_r[pair + t : pair + t + cols_here, :] = spread(
            [e_all[r * nc + t // width + i] for i in range(groups)])[0:NEIGHBORS].T
    len_own = spread([e_all[c * nr + i] for i in range(nr)])
    steps = PIVOT // width
    len_mixed = spread([pick(everyone, p[q] * steps + j) for q in range(2) for j in range(steps)])
    len_r[0:pair, :] = len_mixed[0:NEIGHBORS].T[0:pair, :]
    len_cols = jnp.concatenate([len_own, len_mixed], axis=1)

    def bound_rows(b, carry):
        at = pl.ds(pl.multiple_of(b * PIVOT, PIVOT), PIVOT)
        bounds[at, :] = edge_bound(
            id_ref[at, :], col_ids, ids_r[at, :], len_r[at, :], ids_cols, len_cols)
        return carry

    lax.fori_loop(0, (pair + rows_here) // PIVOT, bound_rows, 0)

    all_of(r_recv, 2).wait_recv()
    rows_panel = jnp.concatenate(
        [pick([r_recv[i, q * PIVOT : (q + 1) * PIVOT, :] for i in range(nr)], row_root[q])
         for q in range(2)], axis=0)
    rows_panel = jnp.minimum(rows_panel, bounds[0:pair, 0:cols_here])
    work[0:pair, :] = rows_panel
    work[pair : 2 * pair, :] = rows_panel
    work[2 * pair :, :] = jnp.minimum(dist[...], bounds[pair:, 0:cols_here])

    all_of(k_all, 4).wait_recv()
    gathered = jnp.concatenate([k_all[i] for i in range(devices)], axis=0)
    for i in range(depth):
        rows = jnp.zeros((levels, cols_here), jnp.float32)
        for part in range(pair // width):
            turned = gathered[part * levels : (part + 1) * levels, :]
            if part != i:
                turned = pltpu.roll(turned, (part - i) * width % cols_here, 1)
            rows = jnp.where(lane // width == part, turned, rows)
        k_ref[pl.ds(i, levels, stride=depth), :] = rows
    corner = k_ref[:, 0:pair]
    corner = jnp.minimum(corner, bounds[0:pair, cols_here : cols_here + pair])
    corner = jnp.concatenate([corner, corner], axis=1)
    corner = lax.fori_loop(0, 6, lambda _, a: square(a, k_ref.at[0:PIVOT, :]), corner)
    left[0:pair, :] = corner

    all_of(c_all, 3).wait_recv()
    cols_packed = jnp.concatenate([c_all[j] for j in range(nc)], axis=0)
    left[pair : pair + half, :] = jnp.minimum(bounds[pair : pair + half, cols_here:], cols_packed)
    left[pair + half :, :] = jnp.minimum(
        bounds[pair + half :, cols_here:], pltpu.roll(cols_packed, pair, 1))

    def finish(b, carry):
        at = pl.ds(pl.multiple_of(b * PIVOT, PIVOT), PIVOT)
        to = pl.ds(pl.multiple_of(pair + b * PIVOT, PIVOT), PIVOT)
        first = jnp.where(b < pair // PIVOT, 0, pair)
        factors = left[at, :]
        total = work[to, :]
        for k in range(pair):
            total = jnp.minimum(total, factors[:, k : k + 1] + work[pl.ds(first + k, 1), :])
        work[to, :] = total
        return carry

    lax.fori_loop(0, (pair + rows_here) // PIVOT, finish, 0)
    out[...] = work[2 * pair :, :]
    for kind, buffer in enumerate([c_recv, e_all, r_recv, c_all, k_all]):
        all_of(buffer, kind).wait_send()


def on_device(nr, nc, distances, neighbor_ids, edge_lengths, pivots):
    rows_here, cols_here = distances.shape
    half = rows_here // 2
    piece = half // nc
    pair = 2 * PIVOT
    depth = pl.next_power_of_2(pl.cdiv(NEIGHBORS, cols_here // edge_lengths.shape[1]))
    vmem = pl.BlockSpec(memory_space=pltpu.VMEM)
    f32 = jnp.float32
    dma = pltpu.SemaphoreType.DMA
    return pl.pallas_call(
        functools.partial(kernel, nr, nc),
        out_shape=jax.ShapeDtypeStruct(distances.shape, f32),
        in_specs=[pl.BlockSpec(memory_space=pltpu.HBM)] * 4,
        out_specs=vmem,
        scratch_shapes=[
            pltpu.SMEM(pivots.shape, jnp.int32),
            pltpu.VMEM(distances.shape, f32),
            pltpu.VMEM(neighbor_ids.shape, jnp.int32),
            pltpu.VMEM(edge_lengths.shape, f32),
            dma((4,)),
            pltpu.VMEM((nr * nc, depth, cols_here), f32),
            pltpu.VMEM((nr * nc, depth, cols_here), f32),
            pltpu.VMEM((pair + rows_here, NEIGHBORS), jnp.int32),
            pltpu.VMEM((pair + rows_here, NEIGHBORS), f32),
            pltpu.VMEM((nc, piece, cols_here), f32),
            pltpu.VMEM((nc, piece, cols_here), f32),
            pltpu.VMEM((nc, piece, cols_here), f32),
            pltpu.VMEM((pair + rows_here, cols_here), f32),
            pltpu.VMEM((nr, 2 * PIVOT, cols_here), f32),
            pltpu.VMEM((nr * nc, 1, cols_here), f32),
            pltpu.VMEM((pair, cols_here), f32),
            pltpu.VMEM((2 * pair + rows_here, cols_here), f32),
            pltpu.VMEM((pair + rows_here, 1), jnp.int32),
            pltpu.VMEM((pair + rows_here, 2 * cols_here), f32),
            dma((5, 2)),
        ],
        compiler_params=pltpu.CompilerParams(
            collective_id=0, has_side_effects=True, vmem_limit_bytes=32 * 1024 * 1024),
    )(*[pltpu.with_memory_space_constraint(x, pltpu.HBM)
        for x in (pivots, distances, neighbor_ids, edge_lengths)])


def solution(mesh):
    placed = (P("row", "col"), P(), P(None, ("row", "col")), P())
    body = functools.partial(on_device, mesh.shape["row"], mesh.shape["col"])
    return jax.shard_map(
        body, mesh=mesh, in_specs=placed, out_specs=P("row", "col"), check_vma=False
    )
```

```python
import functools

import jax
import jax.numpy as jnp
from jax import lax
from jax.experimental import pallas as pl
from jax.experimental.pallas import tpu as pltpu
from jax.sharding import PartitionSpec as P

NEIGHBORS = 10
PIVOT = 32
MESH = pl.DeviceIdType.MESH


def edge_bound(row_ids, col_ids, ids_rows, len_rows, ids_cols, len_cols):
    bound = jnp.where(row_ids == col_ids, jnp.float32(0.0), jnp.inf)
    for k in range(NEIGHBORS):
        forward = jnp.where(ids_rows[:, k : k + 1] == col_ids, len_rows[:, k : k + 1], jnp.inf)
        backward = jnp.where(row_ids == ids_cols[k : k + 1, :], len_cols[k : k + 1, :], jnp.inf)
        bound = jnp.minimum(bound, jnp.minimum(forward, backward))
    return bound


def square(twice, rows_ref):
    size = twice.shape[0]
    lane = lax.broadcasted_iota(jnp.int32, twice.shape, 1)
    rows_ref[...] = jnp.where(lane[: size // 2] < size, twice[: size // 2], twice[size // 2 :])
    total = twice
    for k in range(size // 2):
        inner = jnp.where(lane < size, k, k + size // 2)
        left = jnp.take_along_axis(twice, inner, axis=1, mode="promise_in_bounds")
        total = jnp.minimum(total, left + rows_ref[k : k + 1, :])
    return jnp.minimum(total, pltpu.roll(total, size, 1))


def pick(items, index):
    chosen = items[0]
    index = jnp.full(chosen.shape, index, jnp.int32)
    for i in range(1, len(items)):
        chosen = jnp.where(index == i, items[i], chosen)
    return chosen


def kernel(nr, nc, pivots_in, dist_in, ids_in, lens_in, out, pivots, dist, ids, lens, in_sem,
           e_send, e_all, ids_r, len_r, c_send, c_recv, c_all, left, r_recv, k_all, k_ref, work, id_ref, bounds, sems):
    rows_here, cols_here = dist.shape
    width = lens.shape[1]
    depth = e_all.shape[1]
    groups = cols_here // width
    half = rows_here // 2
    piece = half // nc
    pair = 2 * PIVOT
    devices = nr * nc
    r, c = lax.axis_index("row"), lax.axis_index("col")
    me = r * nc + c
    row_peers = [lax.rem(r + i, nr) for i in range(1, nr)]
    col_peers = [lax.rem(c + i, nc) for i in range(1, nc)]

    barrier = pltpu.get_barrier_semaphore()

    def every_peer(act):
        if devices > 1:

            def step(i, carry):
                other = lax.rem(me + i, devices)
                act(lax.div(other, nc), lax.rem(other, nc))
                return carry

            lax.fori_loop(1, devices, step, 0)
            return
        for i in range(nr):
            for j in range(nc):
                if i or j:
                    act(row_peers[i - 1] if i else r, col_peers[j - 1] if j else c)

    every_peer(lambda row, col: pl.semaphore_signal(
        barrier, inc=1, device_id=(row, col), device_id_type=MESH))

    loads = [
        pltpu.make_async_copy(src, dst, in_sem.at[i])
        for i, (src, dst) in enumerate(
            [(pivots_in, pivots), (dist_in, dist), (lens_in, lens), (ids_in, ids)])
    ]
    for load in loads:
        load.start()
    for load in loads:
        load.wait()
    p = [pivots[q] for q in range(2)]
    base = [p[q] * PIVOT for q in range(2)]
    row_root = [lax.div(base[q], rows_here) for q in range(2)]
    col_root = [lax.div(base[q], cols_here) for q in range(2)]
    row_slot = [lax.rem(p[q], rows_here // PIVOT) for q in range(2)]
    col_slot = [lax.rem(p[q], cols_here // PIVOT) for q in range(2)]
    row_cuts = [slice(i, i + PIVOT) for i in range(0, rows_here, PIVOT)]

    blocks = cols_here // PIVOT
    lane = lax.broadcasted_iota(jnp.int32, (1, cols_here), 1)
    source = jnp.where(
        lane // PIVOT % 2 == 0, jnp.full_like(lane, col_slot[0]), jnp.full_like(lane, col_slot[1]))
    turn = (lane // PIVOT - source + blocks) % blocks
    own_len = jnp.concatenate(
        [lens[...], jnp.zeros((groups * depth - NEIGHBORS, width), jnp.float32)], axis=0)
    own_len = jnp.concatenate(
        [own_len[g * depth : (g + 1) * depth, :] for g in range(groups)], axis=1)
    own_rows = jnp.concatenate(
        [pick([dist[cut, :] for cut in row_cuts], row_slot[q]) for q in range(2)], axis=0)
    r_recv[r] = own_rows
    own_corner = own_rows
    for g in range(1, blocks):
        turned = pltpu.roll(own_rows, g * PIVOT, 1)
        own_corner = jnp.where((turn == g) & (lane < pair), turned, own_corner)
    last = groups - 1
    levels = pair // depth
    for part in range(pair // width):
        turned = pltpu.roll(own_corner, (last - part) * width % cols_here, 1)
        for m in range(levels):
            e_send[part * levels + m] = jnp.where(
                lane // width == last, turned[m * depth : (m + 1) * depth, :], own_len)
    e_all[me] = e_send[me]

    pl.semaphore_wait(barrier, devices - 1)

    def send(src, dst, kind, peer):
        pltpu.make_async_remote_copy(
            src_ref=src, dst_ref=dst, send_sem=sems.at[kind, 0], recv_sem=sems.at[kind, 1],
            device_id=peer, device_id_type=MESH).start()

    def all_of(buffer, kind):
        count = buffer.shape[0] - 1
        every = buffer.at[pl.ds(0, count)]
        return pltpu.make_async_remote_copy(
            src_ref=every, dst_ref=every, send_sem=sems.at[kind, 0], recv_sem=sems.at[kind, 1],
            device_id=(lax.rem(r + 1, nr), c), device_id_type=MESH)

    every_peer(lambda row, col: send(e_send.at[row * nc + col], e_all.at[me], 1, (row, col)))
    packed = jnp.zeros((half, cols_here), jnp.float32)
    for h in range(2):
        part = dist[h * half : (h + 1) * half, :]
        for g in range(blocks):
            turned = pltpu.roll(part, g * PIVOT, 1) if g else part
            packed = jnp.where((turn == g) & (lane // pair == h), turned, packed)
    for j in range(nc):
        c_send[j] = packed[j * piece : (j + 1) * piece, :]
    c_recv[c] = c_send[c]
    for peer in col_peers:
        send(c_send.at[peer], c_recv.at[c], 0, (r, peer))

    for t in range(0, rows_here, cols_here):
        start = pl.multiple_of(r * rows_here + t, cols_here)
        ids_r[pair + t : pair + t + cols_here, :] = ids[:, pl.ds(start, cols_here)].T
    ids_own = ids[:, pl.ds(pl.multiple_of(c * cols_here, cols_here), cols_here)]
    id_tiles = [ids[:, j * cols_here : (j + 1) * cols_here] for j in range(nc)]
    mixed = jnp.zeros_like(ids_own)
    for q in range(2):
        tile = pick(id_tiles, col_root[q])
        for g in range(blocks):
            turned = pltpu.roll(tile, g * PIVOT, 1) if g else tile
            mixed = jnp.where((turn == g) & (lane // PIVOT == q), turned, mixed)
    ids_r[0:pair, :] = mixed.T[0:pair, :]
    ids_cols = jnp.concatenate([ids_own, mixed], axis=1)
    at_s = lax.broadcasted_iota(jnp.int32, (pair, 1), 0)
    id_ref[0:pair, :] = jnp.where(at_s < PIVOT, base[0] + at_s, base[1] + at_s - PIVOT)
    id_ref[pair:, :] = r * rows_here + lax.broadcasted_iota(jnp.int32, (rows_here, 1), 0)
    p_cols = jnp.where(lane < PIVOT, base[0] + lane, base[1] + lane - PIVOT)
    col_ids = jnp.concatenate([c * cols_here + lane, p_cols], axis=1)

    all_of(e_all, 1).wait_recv()
    everyone = [e_all[i] for i in range(devices)]
    in_first_row = lax.rem(me, levels) * depth < PIVOT
    in_first_col = lax.div(me, levels) * width < PIVOT
    owner = (jnp.where(in_first_row, row_root[0], row_root[1]) * nc
             + jnp.where(in_first_col, col_root[0], col_root[1]))
    mine = pick(everyone, owner)
    flat = jnp.zeros((1, cols_here), jnp.float32)
    for i in range(depth):
        turned = mine[i : i + 1, :]
        if i != last:
            turned = pltpu.roll(turned, (i - last) * width % cols_here, 1)
        flat = jnp.where(lane // width == i, turned, flat)
    k_all[me] = flat

    every_peer(lambda row, col: send(k_all.at[me], k_all.at[me], 4, (row, col)))
    for peer in row_peers:
        send(r_recv.at[r], r_recv.at[r], 2, (peer, c))
    all_of(c_recv, 0).wait_recv()
    arrived = [c_recv[j] for j in range(nc)]
    c_all[c] = jnp.where(lane % pair < PIVOT, pick(arrived, col_root[0]), pick(arrived, col_root[1]))
    for peer in col_peers:
        send(c_all.at[c], c_all.at[c], 3, (r, peer))

    def spread(tiles):
        parts = []
        for g in range(-(-NEIGHBORS // depth)):
            part = jnp.zeros((depth, cols_here), jnp.float32)
            for i, tile in enumerate(tiles):
                turned = pltpu.roll(tile, (i - g) * width % cols_here, 1) if i != g else tile
                part = jnp.where(lane // width == i, turned, part)
            parts.append(part)
        return jnp.concatenate(parts, axis=0)

    for t in range(0, rows_here, cols_here):
        len_r[pair + t : pair + t + cols_here, :] = spread(
            [e_all[r * nc + t // width + i] for i in range(groups)])[0:NEIGHBORS].T
    len_own = spread([e_all[c * nr + i] for i in range(nr)])
    steps = PIVOT // width
    len_mixed = spread([pick(everyone, p[q] * steps + j) for q in range(2) for j in range(steps)])
    len_r[0:pair, :] = len_mixed[0:NEIGHBORS].T[0:pair, :]
    len_cols = jnp.concatenate([len_own, len_mixed], axis=1)

    def bound_rows(b, carry):
        at = pl.ds(pl.multiple_of(b * PIVOT, PIVOT), PIVOT)
        bounds[at, :] = edge_bound(
            id_ref[at, :], col_ids, ids_r[at, :], len_r[at, :], ids_cols, len_cols)
        return carry

    lax.fori_loop(0, (pair + rows_here) // PIVOT, bound_rows, 0)

    all_of(r_recv, 2).wait_recv()
    rows_panel = jnp.concatenate(
        [pick([r_recv[i, q * PIVOT : (q + 1) * PIVOT, :] for i in range(nr)], row_root[q])
         for q in range(2)], axis=0)
    rows_panel = jnp.minimum(rows_panel, bounds[0:pair, 0:cols_here])
    work[0:pair, :] = rows_panel
    work[pair : 2 * pair, :] = rows_panel
    work[2 * pair :, :] = jnp.minimum(dist[...], bounds[pair:, 0:cols_here])

    all_of(k_all, 4).wait_recv()
    gathered = jnp.concatenate([k_all[i] for i in range(devices)], axis=0)
    for i in range(depth):
        rows = jnp.zeros((levels, cols_here), jnp.float32)
        for part in range(pair // width):
            turned = gathered[part * levels : (part + 1) * levels, :]
            if part != i:
                turned = pltpu.roll(turned, (part - i) * width % cols_here, 1)
            rows = jnp.where(lane // width == part, turned, rows)
        k_ref[pl.ds(i, levels, stride=depth), :] = rows
    corner = k_ref[:, 0:pair]
    corner = jnp.minimum(corner, bounds[0:pair, cols_here : cols_here + pair])
    corner = jnp.concatenate([corner, corner], axis=1)
    corner = lax.fori_loop(0, 6, lambda _, a: square(a, k_ref.at[0:PIVOT, :]), corner)
    left[0:pair, :] = corner

    all_of(c_all, 3).wait_recv()
    cols_packed = jnp.concatenate([c_all[j] for j in range(nc)], axis=0)
    left[pair : pair + half, :] = jnp.minimum(bounds[pair : pair + half, cols_here:], cols_packed)
    left[pair + half :, :] = jnp.minimum(
        bounds[pair + half :, cols_here:], pltpu.roll(cols_packed, pair, 1))

    def finish(b, carry):
        at = pl.ds(pl.multiple_of(b * pair, pair), pair)
        to = pl.ds(pl.multiple_of(pair + b * pair, pair), pair)
        first = jnp.minimum(b, 1) * pair
        factors = left[at, :]
        total = work[to, :]
        for k in range(pair):
            total = jnp.minimum(total, factors[:, k : k + 1] + work[pl.ds(first + k, 1), :])
        work[to, :] = total
        return carry

    lax.fori_loop(0, (pair + rows_here) // pair, finish, 0)
    out[...] = work[2 * pair :, :]
    for kind, buffer in enumerate([c_recv, e_all, r_recv, c_all, k_all]):
        all_of(buffer, kind).wait_send()


def on_device(nr, nc, distances, neighbor_ids, edge_lengths, pivots):
    rows_here, cols_here = distances.shape
    half = rows_here // 2
    piece = half // nc
    pair = 2 * PIVOT
    depth = pl.next_power_of_2(pl.cdiv(NEIGHBORS, cols_here // edge_lengths.shape[1]))
    vmem = pl.BlockSpec(memory_space=pltpu.VMEM)
    f32 = jnp.float32
    dma = pltpu.SemaphoreType.DMA
    return pl.pallas_call(
        functools.partial(kernel, nr, nc),
        out_shape=jax.ShapeDtypeStruct(distances.shape, f32),
        in_specs=[pl.BlockSpec(memory_space=pltpu.HBM)] * 4,
        out_specs=vmem,
        scratch_shapes=[
            pltpu.SMEM(pivots.shape, jnp.int32),
            pltpu.VMEM(distances.shape, f32),
            pltpu.VMEM(neighbor_ids.shape, jnp.int32),
            pltpu.VMEM(edge_lengths.shape, f32),
            dma((4,)),
            pltpu.VMEM((nr * nc, depth, cols_here), f32),
            pltpu.VMEM((nr * nc, depth, cols_here), f32),
            pltpu.VMEM((pair + rows_here, NEIGHBORS), jnp.int32),
            pltpu.VMEM((pair + rows_here, NEIGHBORS), f32),
            pltpu.VMEM((nc, piece, cols_here), f32),
            pltpu.VMEM((nc, piece, cols_here), f32),
            pltpu.VMEM((nc, piece, cols_here), f32),
            pltpu.VMEM((pair + rows_here, cols_here), f32),
            pltpu.VMEM((nr, 2 * PIVOT, cols_here), f32),
            pltpu.VMEM((nr * nc, 1, cols_here), f32),
            pltpu.VMEM((pair, cols_here), f32),
            pltpu.VMEM((2 * pair + rows_here, cols_here), f32),
            pltpu.VMEM((pair + rows_here, 1), jnp.int32),
            pltpu.VMEM((pair + rows_here, 2 * cols_here), f32),
            dma((5, 2)),
        ],
        compiler_params=pltpu.CompilerParams(
            collective_id=0, has_side_effects=True, vmem_limit_bytes=32 * 1024 * 1024),
    )(*[pltpu.with_memory_space_constraint(x, pltpu.HBM)
        for x in (pivots, distances, neighbor_ids, edge_lengths)])


def solution(mesh):
    placed = (P("row", "col"), P(), P(None, ("row", "col")), P())
    body = functools.partial(on_device, mesh.shape["row"], mesh.shape["col"])
    return jax.shard_map(
        body, mesh=mesh, in_specs=placed, out_specs=P("row", "col"), check_vma=False
    )
```

```python
import functools

import jax
import jax.numpy as jnp
from jax import lax
from jax.experimental import pallas as pl
from jax.experimental.pallas import tpu as pltpu
from jax.sharding import PartitionSpec as P

NEIGHBORS = 10
PIVOT = 32
MESH = pl.DeviceIdType.MESH


def edge_bound(row_ids, col_ids, ids_rows, len_rows, ids_cols, len_cols):
    bound = jnp.where(row_ids == col_ids, jnp.float32(0.0), jnp.inf)
    for k in range(NEIGHBORS):
        forward = jnp.where(ids_rows[:, k : k + 1] == col_ids, len_rows[:, k : k + 1], jnp.inf)
        backward = jnp.where(row_ids == ids_cols[k : k + 1, :], len_cols[k : k + 1, :], jnp.inf)
        bound = jnp.minimum(bound, jnp.minimum(forward, backward))
    return bound


def square(twice, rows_ref):
    size = twice.shape[0]
    lane = lax.broadcasted_iota(jnp.int32, twice.shape, 1)
    rows_ref[...] = jnp.where(lane[: size // 2] < size, twice[: size // 2], twice[size // 2 :])
    total = twice
    for k in range(size // 2):
        inner = jnp.where(lane < size, k, k + size // 2)
        left = jnp.take_along_axis(twice, inner, axis=1, mode="promise_in_bounds")
        total = jnp.minimum(total, left + rows_ref[k : k + 1, :])
    return jnp.minimum(total, pltpu.roll(total, size, 1))


def pick(items, index):
    chosen = items[0]
    index = jnp.full(chosen.shape, index, jnp.int32)
    for i in range(1, len(items)):
        chosen = jnp.where(index == i, items[i], chosen)
    return chosen


def kernel(nr, nc, pivots_in, dist_in, ids_in, lens_in, out, pivots, dist, ids, lens, in_sem,
           e_send, e_all, ids_r, len_r, c_send, c_recv, c_all, left, r_recv, k_all, k_ref, work, id_ref, bounds, sems):
    rows_here, cols_here = dist.shape
    width = lens.shape[1]
    depth = e_all.shape[1]
    groups = cols_here // width
    half = rows_here // 2
    piece = half // nc
    pair = 2 * PIVOT
    devices = nr * nc
    r, c = lax.axis_index("row"), lax.axis_index("col")
    me = r * nc + c
    row_peers = [lax.rem(r + i, nr) for i in range(1, nr)]
    col_peers = [lax.rem(c + i, nc) for i in range(1, nc)]

    barrier = pltpu.get_barrier_semaphore()

    def every_peer(act):
        if devices > 1:

            def step(i, carry):
                other = lax.rem(me + i, devices)
                act(lax.div(other, nc), lax.rem(other, nc))
                return carry

            lax.fori_loop(1, devices, step, 0)
            return
        for i in range(nr):
            for j in range(nc):
                if i or j:
                    act(row_peers[i - 1] if i else r, col_peers[j - 1] if j else c)

    every_peer(lambda row, col: pl.semaphore_signal(
        barrier, inc=1, device_id=(row, col), device_id_type=MESH))

    loads = [
        pltpu.make_async_copy(src, dst, in_sem.at[i])
        for i, (src, dst) in enumerate(
            [(pivots_in, pivots), (dist_in, dist), (lens_in, lens), (ids_in, ids)])
    ]
    for load in loads:
        load.start()
    for load in loads:
        load.wait()
    p = [pivots[q] for q in range(2)]
    base = [p[q] * PIVOT for q in range(2)]
    row_root = [lax.div(base[q], rows_here) for q in range(2)]
    col_root = [lax.div(base[q], cols_here) for q in range(2)]
    row_slot = [lax.rem(p[q], rows_here // PIVOT) for q in range(2)]
    col_slot = [lax.rem(p[q], cols_here // PIVOT) for q in range(2)]
    row_cuts = [slice(i, i + PIVOT) for i in range(0, rows_here, PIVOT)]

    blocks = cols_here // PIVOT
    lane = lax.broadcasted_iota(jnp.int32, (1, cols_here), 1)
    source = jnp.where(
        lane // PIVOT % 2 == 0, jnp.full_like(lane, col_slot[0]), jnp.full_like(lane, col_slot[1]))
    turn = (lane // PIVOT - source + blocks) % blocks
    own_len = jnp.concatenate(
        [lens[...], jnp.zeros((groups * depth - NEIGHBORS, width), jnp.float32)], axis=0)
    own_len = jnp.concatenate(
        [own_len[g * depth : (g + 1) * depth, :] for g in range(groups)], axis=1)
    own_rows = jnp.concatenate(
        [pick([dist[cut, :] for cut in row_cuts], row_slot[q]) for q in range(2)], axis=0)
    r_recv[r] = own_rows
    own_corner = own_rows
    for g in range(1, blocks):
        turned = pltpu.roll(own_rows, g * PIVOT, 1)
        own_corner = jnp.where((turn == g) & (lane < pair), turned, own_corner)
    last = groups - 1
    levels = pair // depth
    for part in range(pair // width):
        turned = pltpu.roll(own_corner, (last - part) * width % cols_here, 1)
        for m in range(levels):
            e_send[part * levels + m] = jnp.where(
                lane // width == last, turned[m * depth : (m + 1) * depth, :], own_len)
    e_all[me] = e_send[me]

    pl.semaphore_wait(barrier, devices - 1)

    def send(src, dst, kind, peer):
        pltpu.make_async_remote_copy(
            src_ref=src, dst_ref=dst, send_sem=sems.at[kind, 0], recv_sem=sems.at[kind, 1],
            device_id=peer, device_id_type=MESH).start()

    def all_of(buffer, kind):
        count = buffer.shape[0] - 1
        every = buffer.at[pl.ds(0, count)]
        return pltpu.make_async_remote_copy(
            src_ref=every, dst_ref=every, send_sem=sems.at[kind, 0], recv_sem=sems.at[kind, 1],
            device_id=(lax.rem(r + 1, nr), c), device_id_type=MESH)

    every_peer(lambda row, col: send(e_send.at[row * nc + col], e_all.at[me], 1, (row, col)))
    packed = jnp.zeros((half, cols_here), jnp.float32)
    for h in range(2):
        part = dist[h * half : (h + 1) * half, :]
        for g in range(blocks):
            turned = pltpu.roll(part, g * PIVOT, 1) if g else part
            packed = jnp.where((turn == g) & (lane // pair == h), turned, packed)
    for j in range(nc):
        c_send[j] = packed[j * piece : (j + 1) * piece, :]
    c_recv[c] = c_send[c]
    for peer in col_peers:
        send(c_send.at[peer], c_recv.at[c], 0, (r, peer))

    for t in range(0, rows_here, cols_here):
        start = pl.multiple_of(r * rows_here + t, cols_here)
        ids_r[pair + t : pair + t + cols_here, :] = ids[:, pl.ds(start, cols_here)].T
    ids_own = ids[:, pl.ds(pl.multiple_of(c * cols_here, cols_here), cols_here)]
    id_tiles = [ids[:, j * cols_here : (j + 1) * cols_here] for j in range(nc)]
    mixed = jnp.zeros_like(ids_own)
    for q in range(2):
        tile = pick(id_tiles, col_root[q])
        for g in range(blocks):
            turned = pltpu.roll(tile, g * PIVOT, 1) if g else tile
            mixed = jnp.where((turn == g) & (lane // PIVOT == q), turned, mixed)
    ids_r[0:pair, :] = mixed.T[0:pair, :]
    ids_cols = jnp.concatenate([ids_own, mixed], axis=1)
    at_s = lax.broadcasted_iota(jnp.int32, (pair, 1), 0)
    id_ref[0:pair, :] = jnp.where(at_s < PIVOT, base[0] + at_s, base[1] + at_s - PIVOT)
    id_ref[pair:, :] = r * rows_here + lax.broadcasted_iota(jnp.int32, (rows_here, 1), 0)
    p_cols = jnp.where(lane < PIVOT, base[0] + lane, base[1] + lane - PIVOT)
    col_ids = jnp.concatenate([c * cols_here + lane, p_cols], axis=1)

    all_of(e_all, 1).wait_recv()
    everyone = [e_all[i] for i in range(devices)]
    in_first_row = lax.rem(me, levels) * depth < PIVOT
    in_first_col = lax.div(me, levels) * width < PIVOT
    owner = (jnp.where(in_first_row, row_root[0], row_root[1]) * nc
             + jnp.where(in_first_col, col_root[0], col_root[1]))
    mine = pick(everyone, owner)
    flat = jnp.zeros((1, cols_here), jnp.float32)
    for i in range(depth):
        turned = mine[i : i + 1, :]
        if i != last:
            turned = pltpu.roll(turned, (i - last) * width % cols_here, 1)
        flat = jnp.where(lane // width == i, turned, flat)
    k_all[me] = flat

    every_peer(lambda row, col: send(k_all.at[me], k_all.at[me], 4, (row, col)))
    for peer in row_peers:
        send(r_recv.at[r], r_recv.at[r], 2, (peer, c))
    def spread(tiles):
        parts = []
        for g in range(-(-NEIGHBORS // depth)):
            part = jnp.zeros((depth, cols_here), jnp.float32)
            for i, tile in enumerate(tiles):
                turned = pltpu.roll(tile, (i - g) * width % cols_here, 1) if i != g else tile
                part = jnp.where(lane // width == i, turned, part)
            parts.append(part)
        return jnp.concatenate(parts, axis=0)

    for t in range(0, rows_here, cols_here):
        len_r[pair + t : pair + t + cols_here, :] = spread(
            [e_all[r * nc + t // width + i] for i in range(groups)])[0:NEIGHBORS].T
    len_own = spread([e_all[c * nr + i] for i in range(nr)])
    steps = PIVOT // width
    len_mixed = spread([pick(everyone, p[q] * steps + j) for q in range(2) for j in range(steps)])
    len_r[0:pair, :] = len_mixed[0:NEIGHBORS].T[0:pair, :]
    len_cols = jnp.concatenate([len_own, len_mixed], axis=1)

    def bound_rows(b, carry):
        at = pl.ds(pl.multiple_of(b * PIVOT, PIVOT), PIVOT)
        bounds[at, :] = edge_bound(
            id_ref[at, :], col_ids, ids_r[at, :], len_r[at, :], ids_cols, len_cols)
        return carry

    lax.fori_loop(0, pair // PIVOT, bound_rows, 0)
    all_of(c_recv, 0).wait_recv()
    arrived = [c_recv[j] for j in range(nc)]
    c_all[c] = jnp.where(lane % pair < PIVOT, pick(arrived, col_root[0]), pick(arrived, col_root[1]))
    for peer in col_peers:
        send(c_all.at[c], c_all.at[c], 3, (r, peer))
    lax.fori_loop(pair // PIVOT, (pair + rows_here) // PIVOT, bound_rows, 0)

    all_of(r_recv, 2).wait_recv()
    rows_panel = jnp.concatenate(
        [pick([r_recv[i, q * PIVOT : (q + 1) * PIVOT, :] for i in range(nr)], row_root[q])
         for q in range(2)], axis=0)
    rows_panel = jnp.minimum(rows_panel, bounds[0:pair, 0:cols_here])
    work[0:pair, :] = rows_panel
    work[pair : 2 * pair, :] = rows_panel
    work[2 * pair :, :] = jnp.minimum(dist[...], bounds[pair:, 0:cols_here])

    all_of(k_all, 4).wait_recv()
    gathered = jnp.concatenate([k_all[i] for i in range(devices)], axis=0)
    for i in range(depth):
        rows = jnp.zeros((levels, cols_here), jnp.float32)
        for part in range(pair // width):
            turned = gathered[part * levels : (part + 1) * levels, :]
            if part != i:
                turned = pltpu.roll(turned, (part - i) * width % cols_here, 1)
            rows = jnp.where(lane // width == part, turned, rows)
        k_ref[pl.ds(i, levels, stride=depth), :] = rows
    corner = k_ref[:, 0:pair]
    corner = jnp.minimum(corner, bounds[0:pair, cols_here : cols_here + pair])
    corner = jnp.concatenate([corner, corner], axis=1)
    corner = lax.fori_loop(0, 6, lambda _, a: square(a, k_ref.at[0:PIVOT, :]), corner)
    left[0:pair, :] = corner

    def finish(b, carry):
        at = pl.ds(pl.multiple_of(b * pair, pair), pair)
        to = pl.ds(pl.multiple_of(pair + b * pair, pair), pair)
        first = jnp.minimum(b, 1) * pair
        factors = left[at, :]
        total = work[to, :]
        for k in range(pair):
            total = jnp.minimum(total, factors[:, k : k + 1] + work[pl.ds(first + k, 1), :])
        work[to, :] = total
        return carry

    lax.fori_loop(0, 1, finish, 0)
    all_of(c_all, 3).wait_recv()
    cols_packed = jnp.concatenate([c_all[j] for j in range(nc)], axis=0)
    left[pair : pair + half, :] = jnp.minimum(bounds[pair : pair + half, cols_here:], cols_packed)
    left[pair + half :, :] = jnp.minimum(
        bounds[pair + half :, cols_here:], pltpu.roll(cols_packed, pair, 1))
    lax.fori_loop(1, (pair + rows_here) // pair, finish, 0)
    out[...] = work[2 * pair :, :]
    for kind, buffer in enumerate([c_recv, e_all, r_recv, c_all, k_all]):
        all_of(buffer, kind).wait_send()


def on_device(nr, nc, distances, neighbor_ids, edge_lengths, pivots):
    rows_here, cols_here = distances.shape
    half = rows_here // 2
    piece = half // nc
    pair = 2 * PIVOT
    depth = pl.next_power_of_2(pl.cdiv(NEIGHBORS, cols_here // edge_lengths.shape[1]))
    vmem = pl.BlockSpec(memory_space=pltpu.VMEM)
    f32 = jnp.float32
    dma = pltpu.SemaphoreType.DMA
    return pl.pallas_call(
        functools.partial(kernel, nr, nc),
        out_shape=jax.ShapeDtypeStruct(distances.shape, f32),
        in_specs=[pl.BlockSpec(memory_space=pltpu.HBM)] * 4,
        out_specs=vmem,
        scratch_shapes=[
            pltpu.SMEM(pivots.shape, jnp.int32),
            pltpu.VMEM(distances.shape, f32),
            pltpu.VMEM(neighbor_ids.shape, jnp.int32),
            pltpu.VMEM(edge_lengths.shape, f32),
            dma((4,)),
            pltpu.VMEM((nr * nc, depth, cols_here), f32),
            pltpu.VMEM((nr * nc, depth, cols_here), f32),
            pltpu.VMEM((pair + rows_here, NEIGHBORS), jnp.int32),
            pltpu.VMEM((pair + rows_here, NEIGHBORS), f32),
            pltpu.VMEM((nc, piece, cols_here), f32),
            pltpu.VMEM((nc, piece, cols_here), f32),
            pltpu.VMEM((nc, piece, cols_here), f32),
            pltpu.VMEM((pair + rows_here, cols_here), f32),
            pltpu.VMEM((nr, 2 * PIVOT, cols_here), f32),
            pltpu.VMEM((nr * nc, 1, cols_here), f32),
            pltpu.VMEM((pair, cols_here), f32),
            pltpu.VMEM((2 * pair + rows_here, cols_here), f32),
            pltpu.VMEM((pair + rows_here, 1), jnp.int32),
            pltpu.VMEM((pair + rows_here, 2 * cols_here), f32),
            dma((5, 2)),
        ],
        compiler_params=pltpu.CompilerParams(
            collective_id=0, has_side_effects=True, vmem_limit_bytes=32 * 1024 * 1024),
    )(*[pltpu.with_memory_space_constraint(x, pltpu.HBM)
        for x in (pivots, distances, neighbor_ids, edge_lengths)])


def solution(mesh):
    placed = (P("row", "col"), P(), P(None, ("row", "col")), P())
    body = functools.partial(on_device, mesh.shape["row"], mesh.shape["col"])
    return jax.shard_map(
        body, mesh=mesh, in_specs=placed, out_specs=P("row", "col"), check_vma=False
    )
```
